32 devices in a mesh: grp: 2 (over y), tile: 16 (over z, x, core).
Axes of the slice: x: 2, y: 2, z: 4, core: 2. Of those that a mesh axis runs over, the one named last changes fastest.
Arguments:
- flux_east: bfloat16 [256, 768, 128], P(None, ('grp', 'tile')), parts along dimension 1, may hold values from -6 to 6
- flux_north: bfloat16 [256, 768, 128], P(None, ('grp', 'tile')), parts along dimension 1, may hold values from -6 to 6
- band_freqs: int32 [96], replicated, may hold values from 1 to 127, as said below
- start_basis: float32 [256, 64], replicated, may hold values from -6 to 6
Outputs:
- rebuilt: bfloat16 [256, 768, 128], P(None, ('grp', 'tile')), parts along dimension 1
The draws below stay inside these ranges and needn't reach their ends.
There are 2 independent parts, one for each index of `grp`. The reference program is written for one: setup_inputs(seed, part) draws one part's arguments, and reference() takes and returns one part's arrays. A program takes and returns all parts, laid end to end along the dimension named above; an argument that names none is the same for every part. Nothing has to cross between parts.
Inputs may be any that keep to these rules, and one draw needn't show every extreme that they name: `band_freqs`: the values are distinct and include 1 and 127.
All inputs are finite; a program needn't handle non-finite values.
Results may differ from the reference program's by a relative error of at most 0.0038.
The reference program's roundings to bfloat16 on the way (of `convergence`, `wave_table`, `bands`, `filtered` and `coefficients`) count: a program that leaves them out, or rounds other values in their place, can miss the bound.
Values may be sent and summed in bfloat16 or wider, within the bound.
No kernel may reach another device: no remote copies, remote signals or barrier semaphores. Data moves between devices by JAX's collectives and lax.ppermute only.
A program may use at most 64 MiB of HBM per device.

```python
import math
import jax
import jax.numpy as jnp
from jax import lax

HOURS = 256
RANK = 64
NBAND = 96
ITERS = 4
CY = 128
NX = 384


def draw_band_freqs(key, part):
    shuffled = jax.random.permutation(key, HOURS // 2 - 3) + 2
    ends = jnp.array([1, HOURS // 2 - 1], dtype=jnp.int32)
    return jnp.concatenate([ends, shuffled[:NBAND - 2].astype(jnp.int32)])


def steps_of(own_key, extent, shards, low, top_value):
    loudness = 1.0
    for dim, parts in shards:
        draws = jax.random.uniform(jax.random.fold_in(jax.random.fold_in(own_key, 6), dim), (parts,), jnp.float32, low / len(shards), top_value / len(shards))
        loudness = loudness * jnp.repeat(jnp.exp(draws), extent[dim] // parts).reshape((-1,) + (1,) * (len(extent) - 1 - dim))
    return loudness


def centred(stream_key, shape, spread, most, shards=(), held_as=jnp.bfloat16):
    gain = steps_of(stream_key, shape, shards, -0.22, 0.18) if shards else 1.0
    drawn = jax.random.normal(stream_key, shape, jnp.float32) * spread * gain
    return jnp.minimum(jnp.maximum(drawn, -most), most).astype(held_as)


def setup_inputs(seed: int = 0, part: int = 0) -> dict:
    seeds = jax.random.split(jax.random.key(seed), 5)
    part_splits = jax.random.split(jax.random.fold_in(seeds[4], part), 5)
    flux_east = centred(part_splits[0], (HOURS, NX, CY), 1.0, 6.0, ((1, 16),))
    flux_north = centred(part_splits[1], (HOURS, NX, CY), 1.0, 6.0, ((1, 16),))
    band_freqs = draw_band_freqs(jax.random.fold_in(seeds[4], 71), part)
    start_basis = centred(seeds[3], (HOURS, RANK), 1.0, 6.0, (), jnp.float32)
    return {"flux_east": flux_east, "flux_north": flux_north, "band_freqs": band_freqs, "start_basis": start_basis}


def wave_table(band_freqs, hour_count):
    times = jnp.arange(hour_count, dtype=jnp.int32)
    phase = times[:, None] * band_freqs[None, :].astype(jnp.int32) % hour_count
    angles = phase.astype(jnp.float32) * (2.0 * math.pi / hour_count)
    return jnp.concatenate([jnp.cos(angles), jnp.sin(angles)], axis=1).astype(jnp.bfloat16)

def refine(gram, basis):
    for sweep in range(ITERS):
        panel = jnp.dot(gram, basis, precision=lax.Precision.HIGHEST)
        crossed = jnp.dot(panel.T, panel, precision=lax.Precision.HIGHEST)
        factor = jnp.linalg.cholesky(crossed)
        basis = jax.scipy.linalg.solve_triangular(factor, panel.T, lower=True).T
    return basis

def reference(flux_east, flux_north, band_freqs, start_basis):
    hour_count, row_count, col_count = flux_east.shape
    eastward = jnp.pad(flux_east.astype(jnp.float32), ((0, 0), (1, 1), (0, 0)))
    northward = jnp.pad(flux_north.astype(jnp.float32), ((0, 0), (0, 0), (1, 1)))
    along = 0.5 * (eastward[:, 2:, :] - eastward[:, :-2, :])
    across = 0.5 * (northward[:, :, 2:] - northward[:, :, :-2])
    convergence = (along + across).astype(jnp.bfloat16).reshape(hour_count, row_count * col_count)
    table = wave_table(band_freqs, hour_count)
    bands = jnp.dot(table.T.astype(jnp.float32), convergence.astype(jnp.float32), preferred_element_type=jnp.float32).astype(jnp.bfloat16)
    filtered = (jnp.dot(table.astype(jnp.float32), bands.astype(jnp.float32), preferred_element_type=jnp.float32) * (2.0 / hour_count)).astype(jnp.bfloat16)
    core = jnp.dot(bands.astype(jnp.float32), bands.T.astype(jnp.float32), preferred_element_type=jnp.float32)
    wide = table.astype(jnp.float32)
    gram = jnp.dot(jnp.dot(wide, core, precision=lax.Precision.HIGHEST), wide.T, precision=lax.Precision.HIGHEST)
    gram = gram * ((2.0 / hour_count) ** 2 / (row_count * col_count))
    basis = refine(gram, start_basis).astype(jnp.bfloat16)
    coefficients = jnp.dot(basis.T.astype(jnp.float32), filtered.astype(jnp.float32), preferred_element_type=jnp.float32).astype(jnp.bfloat16)
    rebuilt = jnp.dot(basis.astype(jnp.float32), coefficients.astype(jnp.float32), preferred_element_type=jnp.float32).astype(jnp.bfloat16)
    return rebuilt.reshape(hour_count, row_count, col_count)
```

```python
import functools
import math

import jax
import jax.numpy as jnp
from jax import lax
from jax.experimental import pallas as pl
from jax.experimental.pallas import tpu as pltpu
from jax.sharding import PartitionSpec as P

ITERS = 4
WIDE = 16
EXACT = lax.Precision.HIGHEST


def partners(count, mask):
    return [(i, i ^ mask) for i in range(count)]


def halo_rows(shard, axis):
    count = lax.axis_size(axis)
    even = lax.axis_index(axis) % 2 == 0
    head, tail = shard[:, :1], shard[:, -1:]
    inner = [(i, i + 1) for i in range(0, count - 1, 2)]
    outer = [(i, i + 1) for i in range(1, count - 1, 2)]
    from_outer = lax.ppermute(
        jnp.where(even, head, tail), axis, outer + [(j, i) for i, j in outer]
    )
    from_inner = lax.ppermute(
        jnp.where(even, tail, head), axis, inner + [(j, i) for i, j in inner]
    )
    before = jnp.where(even, from_outer, from_inner)
    after = jnp.where(even, from_inner, from_outer)
    return before, after


def wave_table(band_freqs, hour_count):
    times = jnp.arange(hour_count, dtype=jnp.int32)
    phase = times[:, None] * band_freqs[None, :] % hour_count
    angles = phase.astype(jnp.float32) * (2.0 * math.pi / hour_count)
    return jnp.concatenate([jnp.cos(angles), jnp.sin(angles)], axis=1).astype(jnp.bfloat16)


def packed(core):
    size = core.shape[0] // 3
    right = jnp.concatenate([core[size:, size : 2 * size], core[2 * size :, 2 * size :]], axis=0)
    return jnp.concatenate([core[:, :size], right], axis=1)


def summed_halves(block, axis):
    count = lax.axis_size(axis)
    half = block.shape[0] // 2
    side = lax.axis_index(axis) % 2
    kept = lax.dynamic_slice_in_dim(block, side * half, half)
    given = lax.dynamic_slice_in_dim(block, (1 - side) * half, half)
    kept = kept + lax.ppermute(given, axis, partners(count, 1))
    mask = 2
    while mask < count:
        kept = kept + lax.ppermute(kept, axis, partners(count, mask))
        mask *= 2
    return kept, lax.ppermute(kept, axis, partners(count, 1))


def exact_dot(a, b):
    return lax.dot_general(
        a, b, (((1,), (0,)), ((), ())), precision=EXACT, preferred_element_type=jnp.float32
    )


def exact_dot_t(a, b):
    return lax.dot_general(
        a, b, (((1,), (1,)), ((), ())), precision=EXACT, preferred_element_type=jnp.float32
    )


def lane(v, j):
    return jnp.broadcast_to(v[:, j : j + 1], v.shape)


def row(v, k):
    return jnp.broadcast_to(v[k : k + 1, :], v.shape)


def reciprocal(x):
    guess = pl.reciprocal(x, approx=True)
    return guess * (2.0 - x * guess)


def inverse_factor(crossed):
    size = crossed.shape[0]
    ids = [lax.broadcasted_iota(jnp.int32, (size, size), d) for d in range(2)]
    eye = (ids[0] == ids[1]).astype(jnp.float32)
    joined = jnp.concatenate([crossed, eye], axis=1)
    strips = [joined[s : s + 8] for s in range(0, size, 8)]
    place = lax.broadcasted_iota(jnp.int32, strips[0].shape, 0)
    rows = []
    for start in range(0, size, WIDE):
        first = start // 8
        cols = [[lane(s, start + k) for s in strips[first:]] for k in range(WIDE)]
        for k in range(0, WIDE, 2):
            q, s = k // 8, k % 8
            a, b, c = row(cols[k][q], s), row(cols[k][q], s + 1), row(cols[k + 1][q], s + 1)
            det = a * c - b * b
            inv = reciprocal(det)
            ai, bi, ci = a * inv, b * inv, c * inv
            below = place > s + 1
            u = [jnp.where(below, cols[k][q], 0.0)] + cols[k][q + 1 :]
            v = [jnp.where(below, cols[k + 1][q], 0.0)] + cols[k + 1][q + 1 :]

            def eliminate(target, offset):
                top, low = row(target[offset], s), row(target[offset], s + 1)
                x, y = ci * top - bi * low, ai * low - bi * top
                for i in range(len(u)):
                    target[offset + i] = target[offset + i] - (u[i] * x + v[i] * y)
                return top, low

            for later in cols[k + 2 :]:
                eliminate(later, q)
            top, low = eliminate(strips, first + q)
            ra = lax.rsqrt(a)
            rows += [top * ra, (a * low - b * top) * (ra * lax.rsqrt(det))]
    out = []
    for s in range(0, size, 8):
        strip = rows[s]
        for k in range(1, 8):
            strip = jnp.where(place == k, rows[s + k], strip)
        out.append(strip)
    return jnp.concatenate(out, axis=0)[:, size:]


def refine_kernel(scale, side_ref, kept_ref, other_ref, start_ref, table_ref, basis_ref):
    kept, other = kept_ref[...], other_ref[...]
    low = side_ref[0] == 0
    both = [jnp.where(low, kept, other), jnp.where(low, other, kept)]
    blocks = jnp.concatenate(both, axis=0) * scale
    size = blocks.shape[1] // 2
    b00, b10, b20 = (blocks[i * size : (i + 1) * size, :size] for i in range(3))
    b11, b21, b22 = (blocks[i * size : (i + 1) * size, size:] for i in range(3))
    core = jnp.concatenate(
        [
            jnp.concatenate([b00, b10.T, b20.T], axis=1),
            jnp.concatenate([b10, b11, b21.T], axis=1),
            jnp.concatenate([b20, b21, b22], axis=1),
        ],
        axis=0,
    )
    wide = table_ref[...].astype(jnp.float32)
    panel = exact_dot_t(exact_dot(start_ref[...], core), wide)
    gram = exact_dot_t(exact_dot(wide, core), wide)
    for sweep in range(ITERS):
        inverse = inverse_factor(exact_dot_t(panel, panel))
        if sweep < ITERS - 1:
            panel = exact_dot(inverse, exact_dot(panel, gram))
    basis_ref[...] = exact_dot(inverse, panel).astype(jnp.bfloat16)


def refine(side, kept, other, start, table, scale):
    vmem = pl.BlockSpec(memory_space=pltpu.VMEM)
    return pl.pallas_call(
        functools.partial(refine_kernel, scale),
        out_shape=jax.ShapeDtypeStruct((start.shape[0], table.shape[0]), jnp.bfloat16),
        in_specs=[pl.BlockSpec(memory_space=pltpu.SMEM)] + [vmem] * 4,
        out_specs=vmem,
        compiler_params=pltpu.CompilerParams(vmem_limit_bytes=32 * 2**20),
        name="refine",
    )(side, kept, other, start, table)


def body(flux_east, flux_north, band_freqs, start_basis):
    hour_count, row_count, col_count = flux_east.shape
    tile_count = lax.axis_size("tile")
    cell_total = row_count * col_count * tile_count
    scale = (2.0 / hour_count) ** 2 / cell_total
    before, after = halo_rows(flux_east, "tile")
    table = wave_table(band_freqs, hour_count)
    start = exact_dot(start_basis.T, table.astype(jnp.float32))
    padded = jnp.concatenate([before, flux_east, after], axis=1)
    northward = jnp.pad(flux_north.astype(jnp.float32), ((0, 0), (0, 0), (1, 1)))
    across = 0.5 * (northward[:, :, 2:] - northward[:, :, :-2])
    eastward = padded.astype(jnp.float32)
    along = 0.5 * (eastward[:, 2:, :] - eastward[:, :-2, :])
    convergence = (along + across).astype(jnp.bfloat16).reshape(hour_count, row_count * col_count)
    bands = jnp.dot(table.T, convergence, preferred_element_type=jnp.float32).astype(jnp.bfloat16)
    filtered = (
        jnp.dot(table, bands, preferred_element_type=jnp.float32) * (2.0 / hour_count)
    ).astype(jnp.bfloat16)
    core = jnp.dot(bands, bands.T, preferred_element_type=jnp.float32)
    kept, other = summed_halves(packed(core), "tile")
    side = (lax.axis_index("tile") % 2).astype(jnp.int32).reshape(1)
    basis_t = refine(side, kept, other, start, table, scale)
    coefficients = jnp.dot(basis_t, filtered, preferred_element_type=jnp.float32).astype(
        jnp.bfloat16
    )
    rebuilt = jnp.dot(basis_t.T, coefficients, preferred_element_type=jnp.float32).astype(
        jnp.bfloat16
    )
    return rebuilt.reshape(hour_count, row_count, col_count)


def solution(mesh):
    placed = (P(None, ("grp", "tile"), None), P(None, ("grp", "tile"), None), P(), P())
    return jax.shard_map(
        body, mesh=mesh, in_specs=placed, out_specs=P(None, ("grp", "tile"), None), check_vma=False
    )
```

```python
import functools
import math

import jax
import jax.numpy as jnp
from jax import lax
from jax.experimental import pallas as pl
from jax.experimental.pallas import tpu as pltpu
from jax.sharding import PartitionSpec as P

ITERS = 4
WIDE = 16
IN_STEPS = 4
OUT_STEPS = 4
INNER_MIB = 60
EXACT = lax.Precision.HIGHEST
VMEM = pl.BlockSpec(memory_space=pltpu.VMEM)
HBM = pl.BlockSpec(memory_space=pltpu.HBM)
MIB = 2**20


def partners(count, mask):
    return [(i, i ^ mask) for i in range(count)]


def parity(index, count):
    bits = index
    shift = 1
    while 1 << shift < count:
        bits = bits ^ (index >> shift)
        shift += 1
    return bits & 1


def wave_table(freqs, hour_count):
    shape = (hour_count, freqs.shape[1])
    times = lax.broadcasted_iota(jnp.int32, shape, 0)
    column = lax.broadcasted_iota(jnp.int32, shape, 1)
    quarter = hour_count // 4
    phase = times * freqs - jnp.where(column < shape[1] // 2, 0, quarter)
    phase = ((phase + 2 * quarter) & (hour_count - 1)) - 2 * quarter
    angle = (quarter - jnp.abs(phase)).astype(jnp.float32) * (2.0 * math.pi / hour_count)
    square = angle * angle
    series = 1.0
    for n in (13, 11, 9, 7, 5, 3):
        series = 1.0 - square * (1.0 / (n * (n - 1))) * series
    return angle * series


def dot(a, b):
    return lax.dot_general(a, b, (((1,), (0,)), ((), ())), preferred_element_type=jnp.float32)


def dot_t(a, b):
    return lax.dot_general(a, b, (((1,), (1,)), ((), ())), preferred_element_type=jnp.float32)


def exact_dot(a, b):
    return lax.dot_general(
        a, b, (((1,), (0,)), ((), ())), precision=EXACT, preferred_element_type=jnp.float32
    )


def exact_dot_t(a, b):
    return lax.dot_general(
        a, b, (((1,), (1,)), ((), ())), precision=EXACT, preferred_element_type=jnp.float32
    )


def cross_band(cols):
    ids = [lax.broadcasted_iota(jnp.int32, (cols, cols), d) for d in range(2)]
    band = jnp.where(ids[0] == ids[1] + 1, 0.5, jnp.where(ids[0] == ids[1] - 1, -0.5, 0.0))
    return band.astype(jnp.bfloat16)


def inner_kernel(
    freqs_ref,
    east_hbm,
    north_hbm,
    bands_ref,
    core_ref,
    edge_ref,
    near_ref,
    far_ref,
    table_ref,
    waves_ref,
    east_ref,
    north_ref,
    along_ref,
    across_ref,
    sems,
):
    hour_count, row_count, cols = east_ref.shape
    steps = sems.shape[0]
    hours = hour_count // steps
    flat = hours * row_count

    def copies(step):
        part = slice(step * hours, (step + 1) * hours)
        return [
            pltpu.make_async_copy(src.at[part], dst.at[part], sems.at[step, k])
            for k, (src, dst) in enumerate(((east_hbm, east_ref), (north_hbm, north_ref)))
        ]

    for step in range(steps):
        for copy in copies(step):
            copy.start()
    freqs = freqs_ref[...]
    table = wave_table(jnp.concatenate([freqs, freqs], axis=1), hour_count)
    waves = table.T.astype(jnp.bfloat16)
    table_ref[...] = table.astype(jnp.bfloat16)
    waves_ref[...] = waves
    band = cross_band(cols)
    for step in range(steps):
        for copy in copies(step):
            copy.wait()
        part = slice(step * hours, (step + 1) * hours)
        to = slice(step * flat, (step + 1) * flat)
        along_ref[to] = 0.5 * east_ref[part].astype(jnp.float32).reshape(flat, cols)
        north = north_ref[part].astype(jnp.float32).reshape(flat, cols).astype(jnp.bfloat16)
        across_ref[to] = dot(north, band)

    def at(ref, i):
        return ref[pl.ds(i, hour_count, stride=row_count)]

    head, tail = at(along_ref, 0) * 2.0, at(along_ref, row_count - 1) * 2.0
    even = lax.axis_index("tile") % 2 == 0
    near_ref[...] = jnp.where(even, tail, head).astype(jnp.bfloat16)
    far_ref[...] = jnp.where(even, head, tail).astype(jnp.bfloat16)
    edge_ref[:, :cols] = at(across_ref, 0) + at(along_ref, 1)
    edge_ref[:, cols:] = at(across_ref, row_count - 1) - at(along_ref, row_count - 2)
    core = None
    for i in range(0, row_count - 2, 2):
        pair = [
            (at(across_ref, k) + (at(along_ref, k + 1) - at(along_ref, k - 1))).astype(jnp.bfloat16)
            for k in (i + 1, i + 2)
        ]
        bands = dot(waves, jnp.concatenate(pair, axis=1)).astype(jnp.bfloat16)
        bands_ref[:, i * cols : (i + 2) * cols] = bands
        product = dot_t(bands, bands)
        core = product if core is None else core + product
    core_ref[...] = core


def inner(freqs, east, north):
    hour_count, row_count, cols = east.shape
    count = 2 * freqs.shape[1]
    f32, bf16 = jnp.float32, jnp.bfloat16
    return pl.pallas_call(
        inner_kernel,
        out_shape=[
            jax.ShapeDtypeStruct((count, (row_count - 2) * cols), bf16),
            jax.ShapeDtypeStruct((count, count), f32),
            jax.ShapeDtypeStruct((hour_count, 2 * cols), f32),
            jax.ShapeDtypeStruct((hour_count, cols), bf16),
            jax.ShapeDtypeStruct((hour_count, cols), bf16),
            jax.ShapeDtypeStruct((hour_count, count), bf16),
            jax.ShapeDtypeStruct((count, hour_count), bf16),
        ],
        in_specs=[VMEM, HBM, HBM],
        out_specs=[VMEM] * 7,
        scratch_shapes=[
            pltpu.VMEM(east.shape, east.dtype),
            pltpu.VMEM(north.shape, north.dtype),
            pltpu.VMEM((hour_count * row_count, cols), f32),
            pltpu.VMEM((hour_count * row_count, cols), f32),
            pltpu.SemaphoreType.DMA((IN_STEPS, 2)),
        ],
        compiler_params=pltpu.CompilerParams(vmem_limit_bytes=INNER_MIB * MIB),
        name="inner",
    )(freqs, east, north)


def outer_kernel(
    tile_count, edge_ref, near_ref, far_ref, waves_ref, core_ref, bands_ref, kept_ref, given_ref
):
    cols = near_ref.shape[1]
    near, far = near_ref[...].astype(jnp.float32), far_ref[...].astype(jnp.float32)
    tile = lax.axis_index("tile")
    far = jnp.where((tile > 0) & (tile < tile_count - 1), far, 0.0)
    even = tile % 2 == 0
    first = edge_ref[:, :cols] - 0.5 * jnp.where(even, far, near)
    final = edge_ref[:, cols:] + 0.5 * jnp.where(even, near, far)
    pair = [first.astype(jnp.bfloat16), final.astype(jnp.bfloat16)]
    bands = dot(waves_ref[...], jnp.concatenate(pair, axis=1)).astype(jnp.bfloat16)
    bands_ref[...] = bands
    core = core_ref[...] + dot_t(bands, bands)
    size = core.shape[0] // 3
    right = jnp.concatenate([core[size:, size : 2 * size], core[2 * size :, 2 * size :]], axis=0)
    packed = jnp.concatenate([core[:, :size], right], axis=1)
    half = packed.shape[0] // 2
    low = parity(tile, tile_count) == 0
    kept_ref[...] = jnp.where(low, packed[:half], packed[half:])
    given_ref[...] = jnp.where(low, packed[half:], packed[:half])


def outer(tile_count, edge, near, far, waves, core):
    count = waves.shape[0]
    half = jax.ShapeDtypeStruct((count // 2, count // 3 * 2), jnp.float32)
    return pl.pallas_call(
        functools.partial(outer_kernel, tile_count),
        out_shape=[jax.ShapeDtypeStruct((count, edge.shape[1]), jnp.bfloat16), half, half],
        in_specs=[VMEM] * 5,
        out_specs=[VMEM] * 3,
        compiler_params=pltpu.CompilerParams(vmem_limit_bytes=16 * MIB),
        name="outer",
    )(edge, near, far, waves, core)


def summed(kept, given, axis, beside):
    count = lax.axis_size(axis)
    kept = kept + lax.ppermute(given, axis, partners(count, 1))
    mask, first = 2, True
    while mask < count:
        kept = kept + lax.ppermute(kept, axis, partners(count, mask + 1))
        if first:
            kept, *beside = lax.optimization_barrier((kept, *beside))
        mask, first = mask * 2, False
    return kept, lax.ppermute(kept, axis, partners(count, 1)), beside


def lane(v, j):
    return jnp.broadcast_to(v[:, j : j + 1], v.shape)


def row(v, k):
    return jnp.broadcast_to(v[k : k + 1, :], v.shape)


def assembled(rows, place):
    strips = []
    for s in range(0, len(rows), 8):
        strip = rows[s]
        for k in range(1, 8):
            strip = jnp.where(place == k, rows[s + k], strip)
        strips.append(strip)
    return jnp.concatenate(strips, axis=0)


def inverse_factor(crossed):
    size = crossed.shape[0]
    ids = [lax.broadcasted_iota(jnp.int32, (size, size), d) for d in range(2)]
    eye = (ids[0] == ids[1]).astype(jnp.float32)
    joined = jnp.concatenate([crossed, eye], axis=1)
    strips = [joined[s : s + 8] for s in range(0, size, 8)]
    place = lax.broadcasted_iota(jnp.int32, strips[0].shape, 0)
    out = []
    for start in range(0, size, WIDE):
        first, last = start // 8, min(size, start + 2 * WIDE) // 8
        cols = [[lane(s, start + k) for s in strips[first:last]] for k in range(WIDE)]
        rows = []
        for k in range(0, WIDE, 2):
            q, s = k // 8, k % 8
            a, b, c = row(cols[k][q], s), row(cols[k][q], s + 1), row(cols[k + 1][q], s + 1)
            det = a * c - b * b
            inv = pl.reciprocal(det, approx=True)
            below = place > s + 1
            u = [jnp.where(below, cols[k][q], 0.0)] + cols[k][q + 1 :]
            v = [jnp.where(below, cols[k + 1][q], 0.0)] + cols[k + 1][q + 1 :]
            x = [i * c - j * b for i, j in zip(u, v)]
            y = [j * a - i * b for i, j in zip(u, v)]

            def eliminate(target, offset):
                top, low = row(target[offset], s), row(target[offset], s + 1)
                top_inv, low_inv = top * inv, low * inv
                for i in range(len(x)):
                    target[offset + i] = (target[offset + i] - x[i] * top_inv) - y[i] * low_inv
                return top, low

            for later in cols[k + 2 :]:
                eliminate(later, q)
            top, low = eliminate(strips, first + q)
            ra = lax.rsqrt(a)
            rows += [top * ra, (a * low - b * top) * (ra * lax.rsqrt(det))]
        out.append(assembled(rows, place))
        if 8 * last < size:
            update = exact_dot(out[-1].T[8 * last : size], out[-1])
            for i in range(last, size // 8):
                strips[i] = strips[i] - update[8 * (i - last) : 8 * (i - last) + 8]
    return jnp.concatenate(out, axis=0)[:, size:]


def thirds(x):
    high = x.astype(jnp.bfloat16)
    rest = x - high.astype(jnp.float32)
    middle = rest.astype(jnp.bfloat16)
    return high, middle, (rest - middle.astype(jnp.float32)).astype(jnp.bfloat16)


def project_kernel(
    scale,
    tile_count,
    kept_ref,
    other_ref,
    start_ref,
    table_ref,
    waves_ref,
    inside_ref,
    edges_ref,
    out_hbm,
    flat_ref,
    out_ref,
    sems,
):
    hour_count, row_count, cols = out_ref.shape
    kept, other = kept_ref[...], other_ref[...]
    low = parity(lax.axis_index("tile"), tile_count) == 0
    blocks = jnp.concatenate([jnp.where(low, kept, other), jnp.where(low, other, kept)], axis=0)
    blocks = blocks * scale
    size = blocks.shape[1] // 2
    b00, b10, b20 = (blocks[i * size : (i + 1) * size, :size] for i in range(3))
    b11, b21, b22 = (blocks[i * size : (i + 1) * size, size:] for i in range(3))
    core = jnp.concatenate(
        [
            jnp.concatenate([b00, b10.T, b20.T], axis=1),
            jnp.concatenate([b10, b11, b21.T], axis=1),
            jnp.concatenate([b20, b21, b22], axis=1),
        ],
        axis=0,
    )
    ids = [lax.broadcasted_iota(jnp.int32, (size, size), d) for d in range(2)]
    trace = jnp.sum(jnp.where(ids[0] == ids[1], b00 + b11 + b22, 0.0), keepdims=True)
    unit = 1.0 / (trace * (hour_count / 2))
    waves = waves_ref[...]

    def by_waves(x):
        high, middle, rest = (dot(part, waves) for part in thirds(x))
        return high + (middle + rest)

    panel = by_waves(exact_dot(start_ref[...], core))
    crossed = exact_dot_t(panel, panel) * unit * unit
    panel = panel * unit
    table = table_ref[...]
    high, middle, rest = (dot(table, part) for part in thirds(by_waves(core)))
    gram = (high + (middle + rest)) * unit
    for sweep in range(ITERS):
        inverse = inverse_factor(crossed)
        if sweep < ITERS - 1:
            panel = exact_dot(inverse, exact_dot(panel, gram))
            crossed = exact_dot_t(panel, panel)
    basis_t = exact_dot(inverse, panel)
    basis = basis_t.T.astype(jnp.bfloat16)
    basis_t = basis_t.astype(jnp.bfloat16)
    parts = [(inside_ref[:, i * cols : (i + 2) * cols], i + 1, i + 2) for i in range(0, row_count - 2, 2)]
    parts.append((edges_ref[...], 0, row_count - 1))
    parts = [(dot(basis_t, part).astype(jnp.bfloat16), rows) for part, *rows in parts]
    steps = sems.shape[0]
    hours = hour_count // steps
    flat = hours * row_count
    copies = []
    for step in range(steps):
        part = slice(step * hours, (step + 1) * hours)
        for coefficients, rows in parts:
            rebuilt = dot(basis[part], coefficients)
            for k, i in enumerate(rows):
                to = pl.ds(step * flat + i, hours, stride=row_count)
                flat_ref[to] = rebuilt[:, k * cols : (k + 1) * cols]
        whole = flat_ref[step * flat : (step + 1) * flat]
        out_ref[part] = whole.reshape(hours, row_count, cols).astype(jnp.bfloat16)
        copies.append(pltpu.make_async_copy(out_ref.at[part], out_hbm.at[part], sems.at[step]))
        copies[-1].start()
    for copy in copies:
        copy.wait()


def project(kept, other, start, table, waves, inside, edges, scale, shape):
    hour_count, row_count, cols = shape
    return pl.pallas_call(
        functools.partial(project_kernel, scale, lax.axis_size("tile")),
        out_shape=jax.ShapeDtypeStruct(shape, jnp.bfloat16),
        in_specs=[VMEM] * 7,
        out_specs=HBM,
        scratch_shapes=[
            pltpu.VMEM((hour_count * row_count, cols), jnp.float32),
            pltpu.VMEM(shape, jnp.bfloat16),
            pltpu.SemaphoreType.DMA((OUT_STEPS,)),
        ],
        compiler_params=pltpu.CompilerParams(vmem_limit_bytes=16 * MIB),
        name="project",
    )(kept, other, start, table, waves, inside, edges)


def body(flux_east, flux_north, band_freqs, start_basis):
    hour_count, row_count, col_count = flux_east.shape
    tile_count = lax.axis_size("tile")
    cell_total = row_count * col_count * tile_count
    scale = (2.0 / hour_count) ** 2 / cell_total
    bands, core, edge, near, far, table, waves = inner(band_freqs[None], flux_east, flux_north)
    near = lax.ppermute(near, "tile", partners(tile_count, 1))
    ring = [(i, (i + (1 if i % 2 else -1)) % tile_count) for i in range(tile_count)]
    far = lax.ppermute(far, "tile", ring)
    start = start_basis.T / jnp.max(jnp.abs(start_basis.T), axis=1, keepdims=True)
    start = exact_dot_t(start, waves.astype(jnp.float32))
    edge_bands, kept, given = outer(tile_count, edge, near, far, waves, core)

    def filtered(part):
        product = jnp.dot(table, part, preferred_element_type=jnp.float32)
        return (product * (2.0 / hour_count)).astype(jnp.bfloat16)

    beside = [filtered(bands), filtered(edge_bands), start]
    kept, other, (inside, edges, start) = summed(kept, given, "tile", beside)
    shape = flux_east.shape
    return project(kept, other, start, table, waves, inside, edges, scale, shape)


def solution(mesh):
    placed = (P(None, ("grp", "tile"), None), P(None, ("grp", "tile"), None), P(), P())
    return jax.shard_map(
        body, mesh=mesh, in_specs=placed, out_specs=P(None, ("grp", "tile"), None), check_vma=False
    )
```

```python
import functools
import math

import jax
import jax.numpy as jnp
from jax import lax
from jax.experimental import pallas as pl
from jax.experimental.pallas import tpu as pltpu
from jax.sharding import PartitionSpec as P

ITERS = 4
WIDE = 16
IN_STEPS = 4
OUT_STEPS = 4
CONVERGE_KIB = 52736
EXACT = lax.Precision.HIGHEST
VMEM = pl.BlockSpec(memory_space=pltpu.VMEM)
HBM = pl.BlockSpec(memory_space=pltpu.HBM)
MIB = 2**20


def partners(count, mask):
    return [(i, i ^ mask) for i in range(count)]


def across_pairs(count, first):
    to = [i ^ 1 for i in range(count)]
    for i in range(2 * first, count - 3, 4):
        for j in range(2):
            to[i + j], to[i + 3 - j] = i + 3 - j, i + j
    return list(enumerate(to))


def parity(index, count):
    bits = index
    shift = 1
    while 1 << shift < count:
        bits = bits ^ (index >> shift)
        shift += 1
    return bits & 1


def wave_table(freqs, hour_count):
    shape = (hour_count, freqs.shape[1])
    times = lax.broadcasted_iota(jnp.int32, shape, 0)
    column = lax.broadcasted_iota(jnp.int32, shape, 1)
    quarter = hour_count // 4
    phase = times * freqs - jnp.where(column < shape[1] // 2, 0, quarter)
    phase = ((phase + 2 * quarter) & (hour_count - 1)) - 2 * quarter
    angle = (quarter - jnp.abs(phase)).astype(jnp.float32) * (2.0 * math.pi / hour_count)
    square = angle * angle
    series = 1.0
    for n in (13, 11, 9, 7, 5, 3):
        series = 1.0 - square * (1.0 / (n * (n - 1))) * series
    return angle * series


def dot(a, b):
    return lax.dot_general(a, b, (((1,), (0,)), ((), ())), preferred_element_type=jnp.float32)


def dot_t(a, b):
    return lax.dot_general(a, b, (((1,), (1,)), ((), ())), preferred_element_type=jnp.float32)


def exact_dot(a, b):
    return lax.dot_general(
        a, b, (((1,), (0,)), ((), ())), precision=EXACT, preferred_element_type=jnp.float32
    )


def exact_dot_t(a, b):
    return lax.dot_general(
        a, b, (((1,), (1,)), ((), ())), precision=EXACT, preferred_element_type=jnp.float32
    )


def cross_band(cols):
    ids = [lax.broadcasted_iota(jnp.int32, (cols, cols), d) for d in range(2)]
    band = jnp.where(ids[0] == ids[1] + 1, 0.5, jnp.where(ids[0] == ids[1] - 1, -0.5, 0.0))
    return band.astype(jnp.bfloat16)


def converge_kernel(
    east_hbm,
    north_hbm,
    inner_ref,
    edge_ref,
    near_ref,
    far_ref,
    east_ref,
    north_ref,
    along_ref,
    across_ref,
    sems,
):
    hour_count, row_count, cols = east_ref.shape
    steps = sems.shape[0]
    hours = hour_count // steps
    flat = hours * row_count
    arrays = ((east_hbm, east_ref), (north_hbm, north_ref))
    parts = [slice(step * hours, (step + 1) * hours) for step in range(steps)]
    copies = [
        [pltpu.make_async_copy(a.at[p], b.at[p], sems.at[i, k]) for k, (a, b) in enumerate(arrays)]
        for i, p in enumerate(parts)
    ]
    for pair in copies:
        for copy in pair:
            copy.start()
    band = cross_band(cols)
    for step, part in enumerate(parts):
        for copy in copies[step]:
            copy.wait()
        to = slice(step * flat, (step + 1) * flat)
        along_ref[to] = 0.5 * east_ref[part].astype(jnp.float32).reshape(flat, cols)
        north = north_ref[part].astype(jnp.float32).reshape(flat, cols).astype(jnp.bfloat16)
        across_ref[to] = dot(north, band)

        def at(ref, i):
            return ref[pl.ds(step * flat + i, hours, stride=row_count)]

        head, tail = at(along_ref, 0) * 2.0, at(along_ref, row_count - 1) * 2.0
        even = lax.axis_index("tile") % 2 == 0
        near_ref[part] = jnp.where(even, tail, head).astype(jnp.bfloat16)
        far_ref[part] = jnp.where(even, head, tail).astype(jnp.bfloat16)
        edge_ref[part, :cols] = at(across_ref, 0) + at(along_ref, 1)
        edge_ref[part, cols:] = at(across_ref, row_count - 1) - at(along_ref, row_count - 2)
        for i in range(1, row_count - 1):
            along = at(along_ref, i + 1) - at(along_ref, i - 1)
            inner_ref[part, (i - 1) * cols : i * cols] = (at(across_ref, i) + along).astype(
                jnp.bfloat16
            )


def converge(east, north):
    hour_count, row_count, cols = east.shape
    f32, bf16 = jnp.float32, jnp.bfloat16
    return pl.pallas_call(
        converge_kernel,
        out_shape=[
            jax.ShapeDtypeStruct((hour_count, (row_count - 2) * cols), bf16),
            jax.ShapeDtypeStruct((hour_count, 2 * cols), f32),
            jax.ShapeDtypeStruct((hour_count, cols), bf16),
            jax.ShapeDtypeStruct((hour_count, cols), bf16),
        ],
        in_specs=[HBM, HBM],
        out_specs=[VMEM] * 4,
        scratch_shapes=[
            pltpu.VMEM(east.shape, east.dtype),
            pltpu.VMEM(north.shape, north.dtype),
            pltpu.VMEM((hour_count * row_count, cols), f32),
            pltpu.VMEM((hour_count * row_count, cols), f32),
            pltpu.SemaphoreType.DMA((IN_STEPS, 2)),
        ],
        compiler_params=pltpu.CompilerParams(vmem_limit_bytes=CONVERGE_KIB * 1024),
        name="converge",
    )(east, north)


def inner_kernel(freqs_ref, inner_ref, bands_ref, core_ref, table_ref, waves_ref):
    hour_count, cells = inner_ref.shape
    freqs = freqs_ref[...]
    table = wave_table(jnp.concatenate([freqs, freqs], axis=1), hour_count)
    waves = table.T.astype(jnp.bfloat16)
    table_ref[...] = table.astype(jnp.bfloat16)
    waves_ref[...] = waves
    core = None
    for i in range(0, cells, 256):
        part = slice(i, i + 256)
        bands = dot(waves, inner_ref[:, part]).astype(jnp.bfloat16)
        bands_ref[:, part] = bands
        product = dot_t(bands, bands)
        core = product if core is None else core + product
    core_ref[...] = core


def inner(freqs, unrounded):
    hour_count, cells = unrounded.shape
    count = 2 * freqs.shape[1]
    f32, bf16 = jnp.float32, jnp.bfloat16
    flops = 2 * count * cells * (hour_count + count)
    return pl.pallas_call(
        inner_kernel,
        out_shape=[
            jax.ShapeDtypeStruct((count, cells), bf16),
            jax.ShapeDtypeStruct((count, count), f32),
            jax.ShapeDtypeStruct((hour_count, count), bf16),
            jax.ShapeDtypeStruct((count, hour_count), bf16),
        ],
        in_specs=[VMEM] * 2,
        out_specs=[VMEM] * 4,
        cost_estimate=pl.CostEstimate(flops=flops, bytes_accessed=6 * MIB, transcendentals=0),
        compiler_params=pltpu.CompilerParams(vmem_limit_bytes=16 * MIB),
        name="inner",
    )(freqs, unrounded)


def outer_kernel(
    tile_count,
    edge_ref,
    near_ref,
    this_ref,
    that_ref,
    waves_ref,
    core_ref,
    bands_ref,
    kept_ref,
    given_ref,
):
    cols = near_ref.shape[1]
    tile = lax.axis_index("tile")
    far = jnp.where((tile // 2 + tile) % 2 == 1, this_ref[...], that_ref[...]).astype(jnp.float32)
    near = near_ref[...].astype(jnp.float32)
    far = jnp.where((tile > 0) & (tile < tile_count - 1), far, 0.0)
    even = tile % 2 == 0
    first = edge_ref[:, :cols] - 0.5 * jnp.where(even, far, near)
    final = edge_ref[:, cols:] + 0.5 * jnp.where(even, near, far)
    pair = [first.astype(jnp.bfloat16), final.astype(jnp.bfloat16)]
    bands = dot(waves_ref[...], jnp.concatenate(pair, axis=1)).astype(jnp.bfloat16)
    bands_ref[...] = bands
    core = core_ref[...] + dot_t(bands, bands)
    size = core.shape[0] // 3
    right = jnp.concatenate([core[size:, size : 2 * size], core[2 * size :, 2 * size :]], axis=0)
    packed = jnp.concatenate([core[:, :size], right], axis=1)
    half = packed.shape[0] // 2
    low = parity(tile, tile_count) == 0
    kept_ref[...] = jnp.where(low, packed[:half], packed[half:])
    given_ref[...] = jnp.where(low, packed[half:], packed[:half])


def outer(tile_count, edge, near, this, that, waves, core):
    count = waves.shape[0]
    half = jax.ShapeDtypeStruct((count // 2, count // 3 * 2), jnp.float32)
    return pl.pallas_call(
        functools.partial(outer_kernel, tile_count),
        out_shape=[jax.ShapeDtypeStruct((count, edge.shape[1]), jnp.bfloat16), half, half],
        in_specs=[VMEM] * 6,
        out_specs=[VMEM] * 3,
        compiler_params=pltpu.CompilerParams(vmem_limit_bytes=16 * MIB),
        name="outer",
    )(edge, near, this, that, waves, core)


def summed(kept, given, axis, beside):
    count = lax.axis_size(axis)
    kept = kept + lax.ppermute(given, axis, partners(count, 1))
    mask, first = 2, True
    while mask < count:
        kept = kept + lax.ppermute(kept, axis, partners(count, mask + 1))
        if first:
            kept, *beside = lax.optimization_barrier((kept, *beside))
        mask, first = mask * 2, False
    return kept, lax.ppermute(kept, axis, partners(count, 1)), beside


def lane(v, j):
    return jnp.broadcast_to(v[:, j : j + 1], v.shape)


def row(v, k):
    return jnp.broadcast_to(v[k : k + 1, :], v.shape)


def assembled(rows, place):
    strips = []
    for s in range(0, len(rows), 8):
        strip = rows[s]
        for k in range(1, 8):
            strip = jnp.where(place == k, rows[s + k], strip)
        strips.append(strip)
    return jnp.concatenate(strips, axis=0)


def inverse_factor(crossed):
    size = crossed.shape[0]
    ids = [lax.broadcasted_iota(jnp.int32, (size, size), d) for d in range(2)]
    eye = (ids[0] == ids[1]).astype(jnp.float32)
    joined = jnp.concatenate([crossed, eye], axis=1)
    strips = [joined[s : s + 8] for s in range(0, size, 8)]
    place = lax.broadcasted_iota(jnp.int32, strips[0].shape, 0)
    out = []
    for start in range(0, size, WIDE):
        first, last = start // 8, min(size, start + 2 * WIDE) // 8
        cols = [[lane(s, start + k) for s in strips[first:last]] for k in range(WIDE)]
        rows = []
        for k in range(0, WIDE, 2):
            q, s = k // 8, k % 8
            a, b, c = row(cols[k][q], s), row(cols[k][q], s + 1), row(cols[k + 1][q], s + 1)
            det = a * c - b * b
            inv = pl.reciprocal(det, approx=True)
            below = place > s + 1
            u = [jnp.where(below, cols[k][q], 0.0)] + cols[k][q + 1 :]
            v = [jnp.where(below, cols[k + 1][q], 0.0)] + cols[k + 1][q + 1 :]
            x = [i * c - j * b for i, j in zip(u, v)]
            y = [j * a - i * b for i, j in zip(u, v)]

            def eliminate(target, offset):
                top, low = row(target[offset], s), row(target[offset], s + 1)
                top_inv, low_inv = top * inv, low * inv
                for i in range(len(x)):
                    target[offset + i] = (target[offset + i] - x[i] * top_inv) - y[i] * low_inv
                return top, low

            for later in cols[k + 2 :]:
                eliminate(later, q)
            top, low = eliminate(strips, first + q)
            ra = lax.rsqrt(a)
            rows += [top * ra, (a * low - b * top) * (ra * lax.rsqrt(det))]
        out.append(assembled(rows, place))
        if 8 * last < size:
            update = exact_dot(out[-1].T[8 * last : size], out[-1])
            for i in range(last, size // 8):
                strips[i] = strips[i] - update[8 * (i - last) : 8 * (i - last) + 8]
    return jnp.concatenate(out, axis=0)[:, size:]


def thirds(x):
    high = x.astype(jnp.bfloat16)
    rest = x - high.astype(jnp.float32)
    middle = rest.astype(jnp.bfloat16)
    return high, middle, (rest - middle.astype(jnp.float32)).astype(jnp.bfloat16)


def project_kernel(
    scale,
    tile_count,
    kept_ref,
    other_ref,
    start_ref,
    table_ref,
    waves_ref,
    inside_ref,
    edges_ref,
    out_hbm,
    flat_ref,
    out_ref,
    sems,
):
    hour_count, row_count, cols = out_ref.shape
    kept, other = kept_ref[...], other_ref[...]
    low = parity(lax.axis_index("tile"), tile_count) == 0
    blocks = jnp.concatenate([jnp.where(low, kept, other), jnp.where(low, other, kept)], axis=0)
    blocks = blocks * scale
    size = blocks.shape[1] // 2
    b00, b10, b20 = (blocks[i * size : (i + 1) * size, :size] for i in range(3))
    b11, b21, b22 = (blocks[i * size : (i + 1) * size, size:] for i in range(3))
    core = jnp.concatenate(
        [
            jnp.concatenate([b00, b10.T, b20.T], axis=1),
            jnp.concatenate([b10, b11, b21.T], axis=1),
            jnp.concatenate([b20, b21, b22], axis=1),
        ],
        axis=0,
    )
    ids = [lax.broadcasted_iota(jnp.int32, (size, size), d) for d in range(2)]
    trace = jnp.sum(jnp.where(ids[0] == ids[1], b00 + b11 + b22, 0.0), keepdims=True)
    unit = 1.0 / (trace * (hour_count / 2))
    waves = waves_ref[...]

    def by_waves(x):
        high, middle, rest = (dot(part, waves) for part in thirds(x))
        return high + (middle + rest)

    panel = by_waves(exact_dot(start_ref[...], core))
    crossed = exact_dot_t(panel, panel) * unit * unit
    panel = panel * unit
    table = table_ref[...]
    high, middle, rest = (dot(table, part) for part in thirds(by_waves(core)))
    gram = (high + (middle + rest)) * unit
    for sweep in range(ITERS):
        inverse = inverse_factor(crossed)
        if sweep < ITERS - 1:
            panel = exact_dot(inverse, exact_dot(panel, gram))
            crossed = exact_dot_t(panel, panel)
    basis_t = exact_dot(inverse, panel)
    basis = basis_t.T.astype(jnp.bfloat16)
    basis_t = basis_t.astype(jnp.bfloat16)
    parts = [(inside_ref[:, i * cols : (i + 2) * cols], i + 1, i + 2) for i in range(0, row_count - 2, 2)]
    parts.append((edges_ref[...], 0, row_count - 1))
    parts = [(dot(basis_t, part).astype(jnp.bfloat16), rows) for part, *rows in parts]
    steps = sems.shape[0]
    hours = hour_count // steps
    flat = hours * row_count
    copies = []
    for step in range(steps):
        part = slice(step * hours, (step + 1) * hours)
        for coefficients, rows in parts:
            rebuilt = dot(basis[part], coefficients)
            for k, i in enumerate(rows):
                to = pl.ds(step * flat + i, hours, stride=row_count)
                flat_ref[to] = rebuilt[:, k * cols : (k + 1) * cols]
        whole = flat_ref[step * flat : (step + 1) * flat]
        out_ref[part] = whole.reshape(hours, row_count, cols).astype(jnp.bfloat16)
        copies.append(pltpu.make_async_copy(out_ref.at[part], out_hbm.at[part], sems.at[step]))
        copies[-1].start()
    for copy in copies:
        copy.wait()


def project(kept, other, start, table, waves, inside, edges, scale, shape):
    hour_count, row_count, cols = shape
    return pl.pallas_call(
        functools.partial(project_kernel, scale, lax.axis_size("tile")),
        out_shape=jax.ShapeDtypeStruct(shape, jnp.bfloat16),
        in_specs=[VMEM] * 7,
        out_specs=HBM,
        scratch_shapes=[
            pltpu.VMEM((hour_count * row_count, cols), jnp.float32),
            pltpu.VMEM(shape, jnp.bfloat16),
            pltpu.SemaphoreType.DMA((OUT_STEPS,)),
        ],
        compiler_params=pltpu.CompilerParams(vmem_limit_bytes=16 * MIB),
        name="project",
    )(kept, other, start, table, waves, inside, edges)


def body(flux_east, flux_north, band_freqs, start_basis):
    hour_count, row_count, col_count = flux_east.shape
    tile_count = lax.axis_size("tile")
    cell_total = row_count * col_count * tile_count
    scale = (2.0 / hour_count) ** 2 / cell_total
    converged, edge, near, far = converge(flux_east, flux_north)
    this = lax.ppermute(far, "tile", across_pairs(tile_count, 0))
    that = lax.ppermute(far, "tile", across_pairs(tile_count, 1))
    near = lax.ppermute(near, "tile", partners(tile_count, 1))
    bands, core, table, waves = inner(band_freqs[None], converged)
    start = start_basis.T / jnp.max(jnp.abs(start_basis.T), axis=1, keepdims=True)
    start = exact_dot_t(start, waves.astype(jnp.float32))
    edge_bands, kept, given = outer(tile_count, edge, near, this, that, waves, core)

    def filtered(part):
        product = jnp.dot(table, part, preferred_element_type=jnp.float32)
        return (product * (2.0 / hour_count)).astype(jnp.bfloat16)

    beside = [filtered(bands), filtered(edge_bands), start]
    kept, other, (inside, edges, start) = summed(kept, given, "tile", beside)
    shape = flux_east.shape
    return project(kept, other, start, table, waves, inside, edges, scale, shape)


def solution(mesh):
    placed = (P(None, ("grp", "tile"), None), P(None, ("grp", "tile"), None), P(), P())
    return jax.shard_map(
        body, mesh=mesh, in_specs=placed, out_specs=P(None, ("grp", "tile"), None), check_vma=False
    )
```

```python
import functools
import math

import jax
import jax.numpy as jnp
from jax import lax
from jax.experimental import pallas as pl
from jax.experimental.pallas import tpu as pltpu
from jax.sharding import PartitionSpec as P

ITERS = 4
WIDE = 8
IN_STEPS = 4
OUT_STEPS = 4
EARLY = 4
CONVERGE_KIB = 52736
VMEM = pl.BlockSpec(memory_space=pltpu.VMEM)
HBM = pl.BlockSpec(memory_space=pltpu.HBM)
MIB = 2**20


def partners(count, mask):
    return [(i, i ^ mask) for i in range(count)]


def across_pairs(count, first):
    to = [i ^ 1 for i in range(count)]
    for i in range(2 * first, count - 3, 4):
        for j in range(2):
            to[i + j], to[i + 3 - j] = i + 3 - j, i + j
    return list(enumerate(to))


def parity(index, count):
    bits = index
    shift = 1
    while 1 << shift < count:
        bits = bits ^ (index >> shift)
        shift += 1
    return bits & 1


def wave_table(freqs, hour_count):
    shape = (hour_count, freqs.shape[1])
    times = lax.broadcasted_iota(jnp.int32, shape, 0)
    column = lax.broadcasted_iota(jnp.int32, shape, 1)
    quarter = hour_count // 4
    phase = times * freqs - jnp.where(column < shape[1] // 2, 0, quarter)
    phase = ((phase + 2 * quarter) & (hour_count - 1)) - 2 * quarter
    angle = (quarter - jnp.abs(phase)).astype(jnp.float32) * (2.0 * math.pi / hour_count)
    square = angle * angle
    series = 1.0
    for n in (13, 11, 9, 7, 5, 3):
        series = 1.0 - square * (1.0 / (n * (n - 1))) * series
    return angle * series


def dot(a, b):
    return lax.dot_general(a, b, (((1,), (0,)), ((), ())), preferred_element_type=jnp.float32)


def dot_t(a, b):
    return lax.dot_general(a, b, (((1,), (1,)), ((), ())), preferred_element_type=jnp.float32)


def thirds(x):
    high = x.astype(jnp.bfloat16)
    rest = x - high.astype(jnp.float32)
    middle = rest.astype(jnp.bfloat16)
    return high, middle, (rest - middle.astype(jnp.float32)).astype(jnp.bfloat16)


def by_thirds(a, b, product):
    n = a.shape[0]
    high, middle, low = thirds(a)
    by_high, by_middle, by_low = thirds(b)
    two = jnp.concatenate([high, middle], axis=0)
    p = product(jnp.concatenate([two, low], axis=0), by_high)
    q, r = product(two, by_middle), product(high, by_low)
    return p[:n] + ((p[n : 2 * n] + q[:n]) + (p[2 * n :] + q[n:] + r))


def exact_dot(a, b):
    return by_thirds(a, b, dot)


def exact_dot_t(a, b):
    return by_thirds(a, b, dot_t)


def cross_band(cols):
    ids = [lax.broadcasted_iota(jnp.int32, (cols, cols), d) for d in range(2)]
    band = jnp.where(ids[0] == ids[1] + 1, 0.5, jnp.where(ids[0] == ids[1] - 1, -0.5, 0.0))
    return band.astype(jnp.bfloat16)


def converge_kernel(
    east_hbm,
    north_hbm,
    inner_ref,
    edge_ref,
    near_ref,
    far_ref,
    east_ref,
    north_ref,
    along_ref,
    across_ref,
    sems,
):
    hour_count, row_count, cols = east_ref.shape
    steps = sems.shape[0]
    hours = hour_count // steps
    flat = hours * row_count
    arrays = ((east_hbm, east_ref), (north_hbm, north_ref))
    parts = [slice(step * hours, (step + 1) * hours) for step in range(steps)]
    copies = [
        [pltpu.make_async_copy(a.at[p], b.at[p], sems.at[i, k]) for k, (a, b) in enumerate(arrays)]
        for i, p in enumerate(parts)
    ]
    for pair in copies:
        for copy in pair:
            copy.start()
    band = cross_band(cols)
    for step, part in enumerate(parts):
        for copy in copies[step]:
            copy.wait()
        to = slice(step * flat, (step + 1) * flat)
        along_ref[to] = 0.5 * east_ref[part].astype(jnp.float32).reshape(flat, cols)
        north = north_ref[part].astype(jnp.float32).reshape(flat, cols).astype(jnp.bfloat16)
        across_ref[to] = dot(north, band)

        def at(ref, i):
            return ref[pl.ds(step * flat + i, hours, stride=row_count)]

        head, tail = at(along_ref, 0) * 2.0, at(along_ref, row_count - 1) * 2.0
        even = lax.axis_index("tile") % 2 == 0
        near_ref[part] = jnp.where(even, tail, head).astype(jnp.bfloat16)
        far_ref[part] = jnp.where(even, head, tail).astype(jnp.bfloat16)
        edge_ref[part, :cols] = at(across_ref, 0) + at(along_ref, 1)
        edge_ref[part, cols:] = at(across_ref, row_count - 1) - at(along_ref, row_count - 2)
        for i in range(1, row_count - 1):
            along = at(along_ref, i + 1) - at(along_ref, i - 1)
            inner_ref[part, (i - 1) * cols : i * cols] = (at(across_ref, i) + along).astype(
                jnp.bfloat16
            )


def converge(east, north):
    hour_count, row_count, cols = east.shape
    f32, bf16 = jnp.float32, jnp.bfloat16
    return pl.pallas_call(
        converge_kernel,
        out_shape=[
            jax.ShapeDtypeStruct((hour_count, (row_count - 2) * cols), bf16),
            jax.ShapeDtypeStruct((hour_count, 2 * cols), f32),
            jax.ShapeDtypeStruct((hour_count, cols), bf16),
            jax.ShapeDtypeStruct((hour_count, cols), bf16),
        ],
        in_specs=[HBM, HBM],
        out_specs=[VMEM] * 4,
        scratch_shapes=[
            pltpu.VMEM(east.shape, east.dtype),
            pltpu.VMEM(north.shape, north.dtype),
            pltpu.VMEM((hour_count * row_count, cols), f32),
            pltpu.VMEM((hour_count * row_count, cols), f32),
            pltpu.SemaphoreType.DMA((IN_STEPS, 2)),
        ],
        compiler_params=pltpu.CompilerParams(vmem_limit_bytes=CONVERGE_KIB * 1024),
        name="converge",
    )(east, north)


def inner_kernel(freqs_ref, inner_ref, bands_ref, core_ref, table_ref, waves_ref):
    hour_count, cells = inner_ref.shape
    freqs = freqs_ref[...]
    table = wave_table(jnp.concatenate([freqs, freqs], axis=1), hour_count)
    waves = table.T.astype(jnp.bfloat16)
    table_ref[...] = table.astype(jnp.bfloat16)
    waves_ref[...] = waves
    core = None
    for i in range(0, cells, 256):
        part = slice(i, i + 256)
        bands = dot(waves, inner_ref[:, part]).astype(jnp.bfloat16)
        bands_ref[:, part] = bands
        product = dot_t(bands, bands)
        core = product if core is None else core + product
    core_ref[...] = core


def inner(freqs, unrounded):
    hour_count, cells = unrounded.shape
    count = 2 * freqs.shape[1]
    f32, bf16 = jnp.float32, jnp.bfloat16
    flops = 2 * count * cells * (hour_count + count)
    return pl.pallas_call(
        inner_kernel,
        out_shape=[
            jax.ShapeDtypeStruct((count, cells), bf16),
            jax.ShapeDtypeStruct((count, count), f32),
            jax.ShapeDtypeStruct((hour_count, count), bf16),
            jax.ShapeDtypeStruct((count, hour_count), bf16),
        ],
        in_specs=[VMEM] * 2,
        out_specs=[VMEM] * 4,
        cost_estimate=pl.CostEstimate(flops=flops, bytes_accessed=6 * MIB, transcendentals=0),
        compiler_params=pltpu.CompilerParams(vmem_limit_bytes=16 * MIB),
        name="inner",
    )(freqs, unrounded)


def outer_kernel(
    tile_count,
    edge_ref,
    near_ref,
    this_ref,
    that_ref,
    waves_ref,
    core_ref,
    bands_ref,
    kept_ref,
    given_ref,
):
    cols = near_ref.shape[1]
    tile = lax.axis_index("tile")
    far = jnp.where((tile // 2 + tile) % 2 == 1, this_ref[...], that_ref[...]).astype(jnp.float32)
    near = near_ref[...].astype(jnp.float32)
    far = jnp.where((tile > 0) & (tile < tile_count - 1), far, 0.0)
    even = tile % 2 == 0
    first = edge_ref[:, :cols] - 0.5 * jnp.where(even, far, near)
    final = edge_ref[:, cols:] + 0.5 * jnp.where(even, near, far)
    pair = [first.astype(jnp.bfloat16), final.astype(jnp.bfloat16)]
    bands = dot(waves_ref[...], jnp.concatenate(pair, axis=1)).astype(jnp.bfloat16)
    bands_ref[...] = bands
    core = core_ref[...] + dot_t(bands, bands)
    size = core.shape[0] // 3
    right = jnp.concatenate([core[size:, size : 2 * size], core[2 * size :, 2 * size :]], axis=0)
    packed = jnp.concatenate([core[:, :size], right], axis=1)
    half = packed.shape[0] // 2
    low = parity(tile, tile_count) == 0
    kept_ref[...] = jnp.where(low, packed[:half], packed[half:])
    given_ref[...] = jnp.where(low, packed[half:], packed[:half])


def outer(tile_count, edge, near, this, that, waves, core):
    count = waves.shape[0]
    half = jax.ShapeDtypeStruct((count // 2, count // 3 * 2), jnp.float32)
    return pl.pallas_call(
        functools.partial(outer_kernel, tile_count),
        out_shape=[jax.ShapeDtypeStruct((count, edge.shape[1]), jnp.bfloat16), half, half],
        in_specs=[VMEM] * 6,
        out_specs=[VMEM] * 3,
        compiler_params=pltpu.CompilerParams(vmem_limit_bytes=16 * MIB),
        name="outer",
    )(edge, near, this, that, waves, core)


def summed(kept, given, axis, beside):
    count = lax.axis_size(axis)
    kept = kept + lax.ppermute(given, axis, partners(count, 1))
    mask, first = 2, True
    while mask < count:
        kept = kept + lax.ppermute(kept, axis, partners(count, mask + 1))
        if first:
            kept, *beside = lax.optimization_barrier((kept, *beside))
        mask, first = mask * 2, False
    return kept, lax.ppermute(kept, axis, partners(count, 1)), beside


def lane(v, j):
    return jnp.take_along_axis(v, jnp.full(v.shape, j, jnp.int32), axis=1)


def row(v, k):
    return jnp.take_along_axis(v, jnp.full(v.shape, k, jnp.int32), axis=0)


def assembled(rows, place):
    strips = []
    for s in range(0, len(rows), 8):
        strip = rows[s]
        for k in range(1, 8):
            strip = jnp.where(place == k, rows[s + k], strip)
        strips.append(strip)
    return jnp.concatenate(strips, axis=0)


def inverse_factor(crossed):
    size = crossed.shape[0]
    ids = [lax.broadcasted_iota(jnp.int32, (size, size), d) for d in range(2)]
    eye = (ids[0] == ids[1]).astype(jnp.float32)
    joined = jnp.concatenate([crossed, eye], axis=1)
    strips = [joined[s : s + 8] for s in range(0, size, 8)]
    place = lax.broadcasted_iota(jnp.int32, strips[0].shape, 0)
    rows, early = [], []
    for start in range(0, size, WIDE):
        first = start // 8
        cols = early + [
            [lane(s, start + k) for s in strips[first:]] for k in range(len(early), WIDE)
        ]
        ahead = range(start + WIDE, min(size, start + WIDE + EARLY))
        early = [[lane(s, j) for s in strips[first:]] for j in ahead]
        for k in range(0, WIDE, 2):
            q, s = k // 8, k % 8
            a, b, c = row(cols[k][q], s), row(cols[k][q], s + 1), row(cols[k + 1][q], s + 1)
            inv_a = pl.reciprocal(a, approx=True)
            m = b * inv_a
            pivot = c - b * m
            inv_c = pl.reciprocal(pivot, approx=True)
            below = place > s + 1
            u = [jnp.where(below, cols[k][q], 0.0)] + cols[k][q + 1 :]
            v = [jnp.where(below, cols[k + 1][q], 0.0)] + cols[k + 1][q + 1 :]
            v = [j - i * m for i, j in zip(u, v)]

            def eliminate(target, offset):
                top, low = row(target[offset], s), row(target[offset], s + 1)
                low = low - top * m
                x, y = top * inv_a, low * inv_c
                for i in range(len(u)):
                    target[offset + i] = (target[offset + i] - u[i] * x) - v[i] * y
                return top, low

            for later in cols[k + 2 :] + early:
                eliminate(later, q)
            top, low = eliminate(strips, first + q)
            rows += [top * lax.rsqrt(a), low * lax.rsqrt(pivot)]
        early = [col[WIDE // 8 :] for col in early]
    return assembled(rows, place)


def stacked(a, b):
    size = a.shape[1] // 2
    left = lax.broadcasted_iota(jnp.int32, a.shape, 1) < size
    high, middle, low = thirds(jnp.where(left, pltpu.roll(a, size, 1), a))
    two = jnp.where(left, high, middle)
    by_high, by_middle, by_low = thirds(b)
    return [
        (
            jnp.concatenate([two, jnp.where(left, high, low)], axis=1),
            jnp.concatenate([by_high, by_high, by_middle, by_high], axis=0),
        ),
        (two, jnp.concatenate([by_low, by_middle], axis=0)),
    ]


def inverse_dot(inverse, b):
    (a, x), (c, y) = stacked(inverse, b)
    return dot(a, x) + dot(c, y)


def project_kernel(
    scale,
    tile_count,
    kept_ref,
    other_ref,
    start_ref,
    table_ref,
    waves_ref,
    inside_ref,
    edges_ref,
    out_hbm,
    flat_ref,
    out_ref,
    sems,
):
    hour_count, row_count, cols = out_ref.shape
    kept, other = kept_ref[...], other_ref[...]
    low = parity(lax.axis_index("tile"), tile_count) == 0
    blocks = jnp.concatenate([jnp.where(low, kept, other), jnp.where(low, other, kept)], axis=0)
    blocks = blocks * scale
    size = blocks.shape[1] // 2
    b00, b10, b20 = (blocks[i * size : (i + 1) * size, :size] for i in range(3))
    b11, b21, b22 = (blocks[i * size : (i + 1) * size, size:] for i in range(3))
    core = jnp.concatenate(
        [
            jnp.concatenate([b00, b10.T, b20.T], axis=1),
            jnp.concatenate([b10, b11, b21.T], axis=1),
            jnp.concatenate([b20, b21, b22], axis=1),
        ],
        axis=0,
    )
    waves = waves_ref[...]

    def by_waves(x):
        high, middle, rest = (dot(part, waves) for part in thirds(x))
        return high + (middle + rest)

    panel = by_waves(exact_dot(start_ref[...], core))
    crossed = exact_dot_t(panel, panel)
    table = table_ref[...]
    high, middle, rest = (dot(table, part) for part in thirds(by_waves(core)))
    gram = high + (middle + rest)
    for sweep in range(ITERS):
        inverse = inverse_factor(crossed)
        if sweep < ITERS - 1:
            panel = inverse_dot(inverse, exact_dot(panel, gram))
            crossed = exact_dot_t(panel, panel)
    basis_t = inverse_dot(inverse, panel)
    basis = basis_t.T.astype(jnp.bfloat16)
    basis_t = basis_t.astype(jnp.bfloat16)
    parts = [(inside_ref[:, i * cols : (i + 2) * cols], i + 1, i + 2) for i in range(0, row_count - 2, 2)]
    parts.append((edges_ref[...], 0, row_count - 1))
    parts = [(dot(basis_t, part).astype(jnp.bfloat16), rows) for part, *rows in parts]
    steps = sems.shape[0]
    hours = hour_count // steps
    flat = hours * row_count
    copies = []
    for step in range(steps):
        part = slice(step * hours, (step + 1) * hours)
        for coefficients, rows in parts:
            rebuilt = dot(basis[part], coefficients)
            for k, i in enumerate(rows):
                to = pl.ds(step * flat + i, hours, stride=row_count)
                flat_ref[to] = rebuilt[:, k * cols : (k + 1) * cols]
        whole = flat_ref[step * flat : (step + 1) * flat]
        out_ref[part] = whole.reshape(hours, row_count, cols).astype(jnp.bfloat16)
        copies.append(pltpu.make_async_copy(out_ref.at[part], out_hbm.at[part], sems.at[step]))
        copies[-1].start()
    for copy in copies:
        copy.wait()


def project(kept, other, start, table, waves, inside, edges, scale, shape):
    hour_count, row_count, cols = shape
    return pl.pallas_call(
        functools.partial(project_kernel, scale, lax.axis_size("tile")),
        out_shape=jax.ShapeDtypeStruct(shape, jnp.bfloat16),
        in_specs=[VMEM] * 7,
        out_specs=HBM,
        scratch_shapes=[
            pltpu.VMEM((hour_count * row_count, cols), jnp.float32),
            pltpu.VMEM(shape, jnp.bfloat16),
            pltpu.SemaphoreType.DMA((OUT_STEPS,)),
        ],
        compiler_params=pltpu.CompilerParams(vmem_limit_bytes=16 * MIB),
        name="project",
    )(kept, other, start, table, waves, inside, edges)


def body(flux_east, flux_north, band_freqs, start_basis):
    hour_count, row_count, col_count = flux_east.shape
    tile_count = lax.axis_size("tile")
    cell_total = row_count * col_count * tile_count
    scale = (2.0 / hour_count) ** 2 / cell_total
    converged, edge, near, far = converge(flux_east, flux_north)
    this = lax.ppermute(far, "tile", across_pairs(tile_count, 0))
    that = lax.ppermute(far, "tile", across_pairs(tile_count, 1))
    near = lax.ppermute(near, "tile", partners(tile_count, 1))
    bands, core, table, waves = inner(band_freqs[None], converged)
    start = jnp.dot(start_basis.T, waves.T.astype(jnp.float32), precision=lax.Precision.HIGHEST)
    edge_bands, kept, given = outer(tile_count, edge, near, this, that, waves, core)

    def filtered(part):
        product = jnp.dot(table, part, preferred_element_type=jnp.float32)
        return (product * (2.0 / hour_count)).astype(jnp.bfloat16)

    beside = [filtered(bands), filtered(edge_bands), start]
    kept, other, (inside, edges, start) = summed(kept, given, "tile", beside)
    shape = flux_east.shape
    return project(kept, other, start, table, waves, inside, edges, scale, shape)


def solution(mesh):
    placed = (P(None, ("grp", "tile"), None), P(None, ("grp", "tile"), None), P(), P())
    return jax.shard_map(
        body, mesh=mesh, in_specs=placed, out_specs=P(None, ("grp", "tile"), None), check_vma=False
    )
```

```python
import functools
import math

import jax
import jax.numpy as jnp
from jax import lax
from jax.experimental import pallas as pl
from jax.experimental.pallas import tpu as pltpu
from jax.sharding import PartitionSpec as P

ITERS = 4
WIDE = 8
IN_STEPS = 4
OUT_STEPS = 4
EARLY = 4
CONVERGE_KIB = 52736
VMEM = pl.BlockSpec(memory_space=pltpu.VMEM)
HBM = pl.BlockSpec(memory_space=pltpu.HBM)
MIB = 2**20


def partners(count, mask):
    return [(i, i ^ mask) for i in range(count)]


def across_pairs(count, first):
    to = [i ^ 1 for i in range(count)]
    for i in range(2 * first, count - 3, 4):
        for j in range(2):
            to[i + j], to[i + 3 - j] = i + 3 - j, i + j
    return list(enumerate(to))


def parity(index, count):
    bits = index
    shift = 1
    while 1 << shift < count:
        bits = bits ^ (index >> shift)
        shift += 1
    return bits & 1


def wave_table(freqs, hour_count):
    shape = (hour_count, freqs.shape[1])
    times = lax.broadcasted_iota(jnp.int32, shape, 0)
    column = lax.broadcasted_iota(jnp.int32, shape, 1)
    quarter = hour_count // 4
    phase = times * freqs - jnp.where(column < shape[1] // 2, 0, quarter)
    phase = ((phase + 2 * quarter) & (hour_count - 1)) - 2 * quarter
    angle = (quarter - jnp.abs(phase)).astype(jnp.float32) * (2.0 * math.pi / hour_count)
    square = angle * angle
    series = 1.0
    for n in (13, 11, 9, 7, 5, 3):
        series = 1.0 - square * (1.0 / (n * (n - 1))) * series
    return angle * series


def dot(a, b):
    return lax.dot_general(a, b, (((1,), (0,)), ((), ())), preferred_element_type=jnp.float32)


def dot_t(a, b):
    return lax.dot_general(a, b, (((1,), (1,)), ((), ())), preferred_element_type=jnp.float32)


def thirds(x):
    high = x.astype(jnp.bfloat16)
    rest = x - high.astype(jnp.float32)
    middle = rest.astype(jnp.bfloat16)
    return high, middle, (rest - middle.astype(jnp.float32)).astype(jnp.bfloat16)


def by_thirds(a, b, product):
    n = a.shape[0]
    high, middle, low = thirds(a)
    by_high, by_middle, by_low = thirds(b)
    two = jnp.concatenate([high, middle], axis=0)
    p = product(jnp.concatenate([two, low], axis=0), by_high)
    q, r = product(two, by_middle), product(high, by_low)
    return p[:n] + ((p[n : 2 * n] + q[:n]) + (p[2 * n :] + q[n:] + r))


def exact_dot(a, b):
    return by_thirds(a, b, dot)


def exact_dot_t(a, b):
    return by_thirds(a, b, dot_t)


def cross_band(cols):
    ids = [lax.broadcasted_iota(jnp.int32, (cols, cols), d) for d in range(2)]
    band = jnp.where(ids[0] == ids[1] + 1, 0.5, jnp.where(ids[0] == ids[1] - 1, -0.5, 0.0))
    return band.astype(jnp.bfloat16)


def converge_kernel(
    east_hbm,
    north_hbm,
    inner_ref,
    edge_ref,
    near_ref,
    far_ref,
    east_ref,
    north_ref,
    along_ref,
    across_ref,
    sems,
):
    hour_count, row_count, cols = east_ref.shape
    steps = sems.shape[0]
    hours = hour_count // steps
    flat = hours * row_count
    arrays = ((east_hbm, east_ref), (north_hbm, north_ref))
    parts = [slice(step * hours, (step + 1) * hours) for step in range(steps)]
    copies = [
        [pltpu.make_async_copy(a.at[p], b.at[p], sems.at[i, k]) for k, (a, b) in enumerate(arrays)]
        for i, p in enumerate(parts)
    ]
    for pair in copies:
        for copy in pair:
            copy.start()
    band = cross_band(cols)
    for step, part in enumerate(parts):
        for copy in copies[step]:
            copy.wait()
        to = slice(step * flat, (step + 1) * flat)
        along_ref[to] = 0.5 * east_ref[part].astype(jnp.float32).reshape(flat, cols)
        north = north_ref[part].astype(jnp.float32).reshape(flat, cols).astype(jnp.bfloat16)
        across_ref[to] = dot(north, band)

        def at(ref, i):
            return ref[pl.ds(step * flat + i, hours, stride=row_count)]

        head, tail = at(along_ref, 0) * 2.0, at(along_ref, row_count - 1) * 2.0
        even = lax.axis_index("tile") % 2 == 0
        near_ref[part] = jnp.where(even, tail, head).astype(jnp.bfloat16)
        far_ref[part] = jnp.where(even, head, tail).astype(jnp.bfloat16)
        edge_ref[part, :cols] = at(across_ref, 0) + at(along_ref, 1)
        edge_ref[part, cols:] = at(across_ref, row_count - 1) - at(along_ref, row_count - 2)
        for i in range(1, row_count - 1):
            along = at(along_ref, i + 1) - at(along_ref, i - 1)
            inner_ref[part, (i - 1) * cols : i * cols] = (at(across_ref, i) + along).astype(
                jnp.bfloat16
            )


def converge(east, north):
    hour_count, row_count, cols = east.shape
    f32, bf16 = jnp.float32, jnp.bfloat16
    return pl.pallas_call(
        converge_kernel,
        out_shape=[
            jax.ShapeDtypeStruct((hour_count, (row_count - 2) * cols), bf16),
            jax.ShapeDtypeStruct((hour_count, 2 * cols), f32),
            jax.ShapeDtypeStruct((hour_count, cols), bf16),
            jax.ShapeDtypeStruct((hour_count, cols), bf16),
        ],
        in_specs=[HBM, HBM],
        out_specs=[VMEM] * 4,
        scratch_shapes=[
            pltpu.VMEM(east.shape, east.dtype),
            pltpu.VMEM(north.shape, north.dtype),
            pltpu.VMEM((hour_count * row_count, cols), f32),
            pltpu.VMEM((hour_count * row_count, cols), f32),
            pltpu.SemaphoreType.DMA((IN_STEPS, 2)),
        ],
        compiler_params=pltpu.CompilerParams(vmem_limit_bytes=CONVERGE_KIB * 1024),
        name="converge",
    )(east, north)


def inner_kernel(freqs_ref, inner_ref, bands_ref, core_ref, table_ref, waves_ref):
    hour_count, cells = inner_ref.shape
    freqs = freqs_ref[...]
    table = wave_table(jnp.concatenate([freqs, freqs], axis=1), hour_count)
    waves = table.T.astype(jnp.bfloat16)
    table_ref[...] = table.astype(jnp.bfloat16)
    waves_ref[...] = waves
    core = None
    for i in range(0, cells, 256):
        part = slice(i, i + 256)
        bands = dot(waves, inner_ref[:, part]).astype(jnp.bfloat16)
        bands_ref[:, part] = bands
        product = dot_t(bands, bands)
        core = product if core is None else core + product
    core_ref[...] = core


def inner(freqs, unrounded):
    hour_count, cells = unrounded.shape
    count = 2 * freqs.shape[1]
    f32, bf16 = jnp.float32, jnp.bfloat16
    flops = 2 * count * cells * (hour_count + count)
    return pl.pallas_call(
        inner_kernel,
        out_shape=[
            jax.ShapeDtypeStruct((count, cells), bf16),
            jax.ShapeDtypeStruct((count, count), f32),
            jax.ShapeDtypeStruct((hour_count, count), bf16),
            jax.ShapeDtypeStruct((count, hour_count), bf16),
        ],
        in_specs=[VMEM] * 2,
        out_specs=[VMEM] * 4,
        cost_estimate=pl.CostEstimate(flops=flops, bytes_accessed=6 * MIB, transcendentals=0),
        compiler_params=pltpu.CompilerParams(vmem_limit_bytes=16 * MIB),
        name="inner",
    )(freqs, unrounded)


def square_ids(size):
    return [lax.broadcasted_iota(jnp.int32, (size, size), d) for d in range(2)]


def pack(core):
    size = core.shape[0] // 3
    b00, b10, b20 = (core[i * size : (i + 1) * size, :size] for i in range(3))
    b11, b21 = (core[i * size : (i + 1) * size, size : 2 * size] for i in (1, 2))
    i, j = square_ids(size)
    diagonal = jnp.sum(jnp.where(i == j, b11, 0.0), axis=0, keepdims=True)
    shared = jnp.where(i >= j, b00, b11)
    third = jnp.where((i == 0) & (j > 0), diagonal, core[2 * size :, 2 * size :])
    third = jnp.where((i == 1) & (j == size - 1), diagonal[:, :1], third)
    half = size // 2
    pairs = ((b10, b20), (b21[:half], b21[half:]), (shared, third))
    return jnp.concatenate([jnp.concatenate(pair, axis=1) for pair in pairs], axis=0)


def unpack(packed):
    size = packed.shape[1] // 2
    half = size // 2
    top, middle, bottom = packed[:size], packed[size : size + half], packed[size + half :]
    b10, b20 = top[:, :size], top[:, size:]
    b21 = jnp.concatenate([middle[:, :size], middle[:, size:]], axis=0)
    shared, third = bottom[:, :size], bottom[:, size:]
    i, j = square_ids(size)
    turned = shared.T
    diagonal = jnp.where(j == 0, third[1:2, size - 1 :], third[:1])
    b00 = jnp.where(i >= j, shared, turned)
    b11 = jnp.where(i < j, shared, jnp.where(i > j, turned, diagonal))
    b22 = jnp.where(i >= j, third, third.T)
    rows = ((b00, b10.T, b20.T), (b10, b11, b21.T), (b20, b21, b22))
    return jnp.concatenate([jnp.concatenate(row, axis=1) for row in rows], axis=0)


def outer_kernel(
    tile_count,
    edge_ref,
    near_ref,
    this_ref,
    that_ref,
    waves_ref,
    core_ref,
    bands_ref,
    kept_ref,
    given_ref,
):
    cols = near_ref.shape[1]
    tile = lax.axis_index("tile")
    far = jnp.where((tile // 2 + tile) % 2 == 1, this_ref[...], that_ref[...]).astype(jnp.float32)
    near = near_ref[...].astype(jnp.float32)
    far = jnp.where((tile > 0) & (tile < tile_count - 1), far, 0.0)
    even = tile % 2 == 0
    first = edge_ref[:, :cols] - 0.5 * jnp.where(even, far, near)
    final = edge_ref[:, cols:] + 0.5 * jnp.where(even, near, far)
    pair = [first.astype(jnp.bfloat16), final.astype(jnp.bfloat16)]
    bands = dot(waves_ref[...], jnp.concatenate(pair, axis=1)).astype(jnp.bfloat16)
    bands_ref[...] = bands
    core = core_ref[...] + dot_t(bands, bands)
    packed = pack(core)
    half = packed.shape[0] // 2
    low = parity(tile, tile_count) == 0
    kept_ref[...] = jnp.where(low, packed[:half], packed[half:])
    given_ref[...] = jnp.where(low, packed[half:], packed[:half])


def outer(tile_count, edge, near, this, that, waves, core):
    count = waves.shape[0]
    half = jax.ShapeDtypeStruct((count // 12 * 5, count // 3 * 2), jnp.float32)
    return pl.pallas_call(
        functools.partial(outer_kernel, tile_count),
        out_shape=[jax.ShapeDtypeStruct((count, edge.shape[1]), jnp.bfloat16), half, half],
        in_specs=[VMEM] * 6,
        out_specs=[VMEM] * 3,
        compiler_params=pltpu.CompilerParams(vmem_limit_bytes=16 * MIB),
        name="outer",
    )(edge, near, this, that, waves, core)


def summed(kept, given, axis, beside):
    count = lax.axis_size(axis)
    kept = kept + lax.ppermute(given, axis, partners(count, 1))
    mask, first = 2, True
    while mask < count:
        kept = kept + lax.ppermute(kept, axis, partners(count, mask + 1))
        if first:
            kept, *beside = lax.optimization_barrier((kept, *beside))
        mask, first = mask * 2, False
    return kept, lax.ppermute(kept, axis, partners(count, 1)), beside


def lane(v, j):
    return jnp.take_along_axis(v, jnp.full(v.shape, j, jnp.int32), axis=1)


def row(v, k):
    return jnp.take_along_axis(v, jnp.full(v.shape, k, jnp.int32), axis=0)


def assembled(rows, place):
    strips = []
    for s in range(0, len(rows), 8):
        strip = rows[s]
        for k in range(1, 8):
            strip = jnp.where(place == k, rows[s + k], strip)
        strips.append(strip)
    return jnp.concatenate(strips, axis=0)


def inverse_factor(crossed):
    size = crossed.shape[0]
    ids = [lax.broadcasted_iota(jnp.int32, (size, size), d) for d in range(2)]
    eye = (ids[0] == ids[1]).astype(jnp.float32)
    joined = jnp.concatenate([crossed, eye], axis=1)
    strips = [joined[s : s + 8] for s in range(0, size, 8)]
    place = lax.broadcasted_iota(jnp.int32, strips[0].shape, 0)
    rows, early = [], []
    for start in range(0, size, WIDE):
        first = start // 8
        cols = early + [
            [lane(s, start + k) for s in strips[first:]] for k in range(len(early), WIDE)
        ]
        ahead = range(start + WIDE, min(size, start + WIDE + EARLY))
        early = [[lane(s, j) for s in strips[first:]] for j in ahead]
        for k in range(0, WIDE, 2):
            q, s = k // 8, k % 8
            a, b, c = row(cols[k][q], s), row(cols[k][q], s + 1), row(cols[k + 1][q], s + 1)
            inv_a = pl.reciprocal(a, approx=True)
            m = b * inv_a
            pivot = c - b * m
            inv_c = pl.reciprocal(pivot, approx=True)
            below = place > s + 1
            u = [jnp.where(below, cols[k][q], 0.0)] + cols[k][q + 1 :]
            v = [jnp.where(below, cols[k + 1][q], 0.0)] + cols[k + 1][q + 1 :]
            v = [j - i * m for i, j in zip(u, v)]

            def eliminate(target, offset):
                top, low = row(target[offset], s), row(target[offset], s + 1)
                low = low - top * m
                x, y = top * inv_a, low * inv_c
                for i in range(len(u)):
                    target[offset + i] = (target[offset + i] - u[i] * x) - v[i] * y
                return top, low

            for later in cols[k + 2 :] + early:
                eliminate(later, q)
            top, low = eliminate(strips, first + q)
            rows += [top * lax.rsqrt(a), low * lax.rsqrt(pivot)]
        early = [col[WIDE // 8 :] for col in early]
    return assembled(rows, place)


def stacked(a, b):
    size = a.shape[1] // 2
    left = lax.broadcasted_iota(jnp.int32, a.shape, 1) < size
    high, middle, low = thirds(jnp.where(left, pltpu.roll(a, size, 1), a))
    two = jnp.where(left, high, middle)
    by_high, by_middle, by_low = thirds(b)
    return [
        (
            jnp.concatenate([two, jnp.where(left, high, low)], axis=1),
            jnp.concatenate([by_high, by_high, by_middle, by_high], axis=0),
        ),
        (two, jnp.concatenate([by_low, by_middle], axis=0)),
    ]


def inverse_dot(inverse, b):
    (a, x), (c, y) = stacked(inverse, b)
    return dot(a, x) + dot(c, y)


def project_kernel(
    scale,
    tile_count,
    kept_ref,
    other_ref,
    start_ref,
    table_ref,
    waves_ref,
    inside_ref,
    edges_ref,
    out_hbm,
    flat_ref,
    out_ref,
    sems,
):
    hour_count, row_count, cols = out_ref.shape
    kept, other = kept_ref[...], other_ref[...]
    low = parity(lax.axis_index("tile"), tile_count) == 0
    blocks = jnp.concatenate([jnp.where(low, kept, other), jnp.where(low, other, kept)], axis=0)
    core = unpack(blocks * scale)
    waves = waves_ref[...]

    def by_waves(x):
        high, middle, rest = (dot(part, waves) for part in thirds(x))
        return high + (middle + rest)

    panel = by_waves(exact_dot(start_ref[...], core))
    crossed = exact_dot_t(panel, panel)
    table = table_ref[...]
    high, middle, rest = (dot(table, part) for part in thirds(by_waves(core)))
    gram = high + (middle + rest)
    for sweep in range(ITERS):
        inverse = inverse_factor(crossed)
        if sweep < ITERS - 1:
            panel = inverse_dot(inverse, exact_dot(panel, gram))
            crossed = exact_dot_t(panel, panel)
    basis_t = inverse_dot(inverse, panel)
    basis = basis_t.T.astype(jnp.bfloat16)
    basis_t = basis_t.astype(jnp.bfloat16)
    parts = [(inside_ref[:, i * cols : (i + 2) * cols], i + 1, i + 2) for i in range(0, row_count - 2, 2)]
    parts.append((edges_ref[...], 0, row_count - 1))
    parts = [(dot(basis_t, part).astype(jnp.bfloat16), rows) for part, *rows in parts]
    steps = sems.shape[0]
    hours = hour_count // steps
    flat = hours * row_count
    copies = []
    for step in range(steps):
        part = slice(step * hours, (step + 1) * hours)
        for coefficients, rows in parts:
            rebuilt = dot(basis[part], coefficients)
            for k, i in enumerate(rows):
                to = pl.ds(step * flat + i, hours, stride=row_count)
                flat_ref[to] = rebuilt[:, k * cols : (k + 1) * cols]
        whole = flat_ref[step * flat : (step + 1) * flat]
        out_ref[part] = whole.reshape(hours, row_count, cols).astype(jnp.bfloat16)
        copies.append(pltpu.make_async_copy(out_ref.at[part], out_hbm.at[part], sems.at[step]))
        copies[-1].start()
    for copy in copies:
        copy.wait()


def project(kept, other, start, table, waves, inside, edges, scale, shape):
    hour_count, row_count, cols = shape
    return pl.pallas_call(
        functools.partial(project_kernel, scale, lax.axis_size("tile")),
        out_shape=jax.ShapeDtypeStruct(shape, jnp.bfloat16),
        in_specs=[VMEM] * 7,
        out_specs=HBM,
        scratch_shapes=[
            pltpu.VMEM((hour_count * row_count, cols), jnp.float32),
            pltpu.VMEM(shape, jnp.bfloat16),
            pltpu.SemaphoreType.DMA((OUT_STEPS,)),
        ],
        compiler_params=pltpu.CompilerParams(vmem_limit_bytes=16 * MIB),
        name="project",
    )(kept, other, start, table, waves, inside, edges)


def body(flux_east, flux_north, band_freqs, start_basis):
    hour_count, row_count, col_count = flux_east.shape
    tile_count = lax.axis_size("tile")
    cell_total = row_count * col_count * tile_count
    scale = (2.0 / hour_count) ** 2 / cell_total
    converged, edge, near, far = converge(flux_east, flux_north)
    this = lax.ppermute(far, "tile", across_pairs(tile_count, 0))
    that = lax.ppermute(far, "tile", across_pairs(tile_count, 1))
    near = lax.ppermute(near, "tile", partners(tile_count, 1))
    bands, core, table, waves = inner(band_freqs[None], converged)
    start = jnp.dot(start_basis.T, waves.T.astype(jnp.float32), precision=lax.Precision.HIGHEST)
    edge_bands, kept, given = outer(tile_count, edge, near, this, that, waves, core)

    def filtered(part):
        product = jnp.dot(table, part, preferred_element_type=jnp.float32)
        return (product * (2.0 / hour_count)).astype(jnp.bfloat16)

    beside = [filtered(bands), filtered(edge_bands), start]
    kept, other, (inside, edges, start) = summed(kept, given, "tile", beside)
    shape = flux_east.shape
    return project(kept, other, start, table, waves, inside, edges, scale, shape)


def solution(mesh):
    placed = (P(None, ("grp", "tile"), None), P(None, ("grp", "tile"), None), P(), P())
    return jax.shard_map(
        body, mesh=mesh, in_specs=placed, out_specs=P(None, ("grp", "tile"), None), check_vma=False
    )
```

```python
import functools
import math

import jax
import jax.numpy as jnp
from jax import lax
from jax.experimental import pallas as pl
from jax.experimental.pallas import tpu as pltpu
from jax.sharding import PartitionSpec as P

ITERS = 4
WIDE = 8
IN_STEPS = 4
OUT_STEPS = 4
EARLY = 4
CONVERGE_KIB = 52736
VMEM = pl.BlockSpec(memory_space=pltpu.VMEM)
HBM = pl.BlockSpec(memory_space=pltpu.HBM)
MIB = 2**20


def partners(count, mask):
    return [(i, i ^ mask) for i in range(count)]


def across_pairs(count, first):
    to = [i ^ 1 for i in range(count)]
    for i in range(2 * first, count - 3, 4):
        for j in range(2):
            to[i + j], to[i + 3 - j] = i + 3 - j, i + j
    return list(enumerate(to))


def parity(index, count):
    bits = index
    shift = 1
    while 1 << shift < count:
        bits = bits ^ (index >> shift)
        shift += 1
    return bits & 1


def wave_table(freqs, hour_count):
    shape = (hour_count, freqs.shape[1])
    times = lax.broadcasted_iota(jnp.int32, shape, 0)
    column = lax.broadcasted_iota(jnp.int32, shape, 1)
    quarter = hour_count // 4
    phase = times * freqs - jnp.where(column < shape[1] // 2, 0, quarter)
    phase = ((phase + 2 * quarter) & (hour_count - 1)) - 2 * quarter
    angle = (quarter - jnp.abs(phase)).astype(jnp.float32) * (2.0 * math.pi / hour_count)
    square = angle * angle
    series = 1.0
    for n in (13, 11, 9, 7, 5, 3):
        series = 1.0 - square * (1.0 / (n * (n - 1))) * series
    return angle * series


def dot(a, b):
    return lax.dot_general(a, b, (((1,), (0,)), ((), ())), preferred_element_type=jnp.float32)


def dot_t(a, b):
    return lax.dot_general(a, b, (((1,), (1,)), ((), ())), preferred_element_type=jnp.float32)


def thirds(x):
    high = x.astype(jnp.bfloat16)
    rest = x - high.astype(jnp.float32)
    middle = rest.astype(jnp.bfloat16)
    return high, middle, (rest - middle.astype(jnp.float32)).astype(jnp.bfloat16)


def by_thirds(a, b, product):
    n = a.shape[0]
    high, middle, low = thirds(a)
    by_high, by_middle, by_low = thirds(b)
    two = jnp.concatenate([high, middle], axis=0)
    p = product(jnp.concatenate([two, low], axis=0), by_high)
    q, r = product(two, by_middle), product(high, by_low)
    return p[:n] + ((p[n : 2 * n] + q[:n]) + (p[2 * n :] + q[n:] + r))


def exact_dot(a, b):
    return by_thirds(a, b, dot)


def exact_dot_t(a, b):
    return by_thirds(a, b, dot_t)


def cross_band(cols):
    ids = [lax.broadcasted_iota(jnp.int32, (cols, cols), d) for d in range(2)]
    band = jnp.where(ids[0] == ids[1] + 1, 0.5, jnp.where(ids[0] == ids[1] - 1, -0.5, 0.0))
    return band.astype(jnp.bfloat16)


def inner_kernel(
    freqs_ref,
    east_hbm,
    north_hbm,
    bands_ref,
    core_ref,
    edge_ref,
    table_ref,
    waves_ref,
    east_ref,
    north_ref,
    along_ref,
    across_ref,
    inner_ref,
    sems,
):
    hour_count, row_count, cols = east_ref.shape
    steps = sems.shape[0]
    hours = hour_count // steps
    flat = hours * row_count

    def copies(step):
        part = slice(step * hours, (step + 1) * hours)
        return [
            pltpu.make_async_copy(src.at[part], dst.at[part], sems.at[step, k])
            for k, (src, dst) in enumerate(((east_hbm, east_ref), (north_hbm, north_ref)))
        ]

    for step in range(steps):
        for copy in copies(step):
            copy.start()
    freqs = freqs_ref[...]
    table = wave_table(jnp.concatenate([freqs, freqs], axis=1), hour_count)
    waves = table.T.astype(jnp.bfloat16)
    table_ref[...] = table.astype(jnp.bfloat16)
    waves_ref[...] = waves
    band = cross_band(cols)
    for step in range(steps):
        for copy in copies(step):
            copy.wait()
        part = slice(step * hours, (step + 1) * hours)
        to = slice(step * flat, (step + 1) * flat)
        along_ref[to] = 0.5 * east_ref[part].astype(jnp.float32).reshape(flat, cols)
        north = north_ref[part].astype(jnp.float32).reshape(flat, cols).astype(jnp.bfloat16)
        across_ref[to] = dot(north, band)


        def at(ref, i):
            return ref[pl.ds(step * flat + i, hours, stride=row_count)]

        edge_ref[part, :cols] = at(across_ref, 0) + at(along_ref, 1)
        edge_ref[part, cols:] = at(across_ref, row_count - 1) - at(along_ref, row_count - 2)
        for i in range(1, row_count - 1):
            along = at(along_ref, i + 1) - at(along_ref, i - 1)
            inner_ref[part, (i - 1) * cols : i * cols] = (at(across_ref, i) + along).astype(
                jnp.bfloat16
            )
    core = None
    for i in range(0, row_count - 2, 2):
        pair = slice(i * cols, (i + 2) * cols)
        bands = dot(waves, inner_ref[:, pair]).astype(jnp.bfloat16)
        bands_ref[:, pair] = bands
        product = dot_t(bands, bands)
        core = product if core is None else core + product
    core_ref[...] = core


def inner(freqs, east, north):
    hour_count, row_count, cols = east.shape
    count = 2 * freqs.shape[1]
    f32, bf16 = jnp.float32, jnp.bfloat16
    return pl.pallas_call(
        inner_kernel,
        out_shape=[
            jax.ShapeDtypeStruct((count, (row_count - 2) * cols), bf16),
            jax.ShapeDtypeStruct((count, count), f32),
            jax.ShapeDtypeStruct((hour_count, 2 * cols), f32),
            jax.ShapeDtypeStruct((hour_count, count), bf16),
            jax.ShapeDtypeStruct((count, hour_count), bf16),
        ],
        in_specs=[VMEM, HBM, HBM],
        out_specs=[VMEM] * 5,
        scratch_shapes=[
            pltpu.VMEM(east.shape, east.dtype),
            pltpu.VMEM(north.shape, north.dtype),
            pltpu.VMEM((hour_count * row_count, cols), f32),
            pltpu.VMEM((hour_count * row_count, cols), f32),
            pltpu.VMEM((hour_count, (row_count - 2) * cols), bf16),
            pltpu.SemaphoreType.DMA((IN_STEPS, 2)),
        ],
        compiler_params=pltpu.CompilerParams(vmem_limit_bytes=CONVERGE_KIB * 1024),
        name="inner",
    )(freqs, east, north)


def square_ids(size):
    return [lax.broadcasted_iota(jnp.int32, (size, size), d) for d in range(2)]


def pack(core):
    size = core.shape[0] // 3
    b00, b10, b20 = (core[i * size : (i + 1) * size, :size] for i in range(3))
    b11, b21 = (core[i * size : (i + 1) * size, size : 2 * size] for i in (1, 2))
    i, j = square_ids(size)
    diagonal = jnp.sum(jnp.where(i == j, b11, 0.0), axis=0, keepdims=True)
    shared = jnp.where(i >= j, b00, b11)
    third = jnp.where((i == 0) & (j > 0), diagonal, core[2 * size :, 2 * size :])
    third = jnp.where((i == 1) & (j == size - 1), diagonal[:, :1], third)
    half = size // 2
    pairs = ((b10, b20), (b21[:half], b21[half:]), (shared, third))
    return jnp.concatenate([jnp.concatenate(pair, axis=1) for pair in pairs], axis=0)


def unpack(packed):
    size = packed.shape[1] // 2
    half = size // 2
    top, middle, bottom = packed[:size], packed[size : size + half], packed[size + half :]
    b10, b20 = top[:, :size], top[:, size:]
    b21 = jnp.concatenate([middle[:, :size], middle[:, size:]], axis=0)
    shared, third = bottom[:, :size], bottom[:, size:]
    i, j = square_ids(size)
    turned = shared.T
    diagonal = jnp.where(j == 0, third[1:2, size - 1 :], third[:1])
    b00 = jnp.where(i >= j, shared, turned)
    b11 = jnp.where(i < j, shared, jnp.where(i > j, turned, diagonal))
    b22 = jnp.where(i >= j, third, third.T)
    rows = ((b00, b10.T, b20.T), (b10, b11, b21.T), (b20, b21, b22))
    return jnp.concatenate([jnp.concatenate(row, axis=1) for row in rows], axis=0)


def outer_kernel(
    tile_count,
    edge_ref,
    near_ref,
    this_ref,
    that_ref,
    waves_ref,
    core_ref,
    bands_ref,
    kept_ref,
    given_ref,
):
    cols = near_ref.shape[1]
    tile = lax.axis_index("tile")
    far = jnp.where((tile // 2 + tile) % 2 == 1, this_ref[...], that_ref[...]).astype(jnp.float32)
    near = near_ref[...].astype(jnp.float32)
    far = jnp.where((tile > 0) & (tile < tile_count - 1), far, 0.0)
    even = tile % 2 == 0
    first = edge_ref[:, :cols] - 0.5 * jnp.where(even, far, near)
    final = edge_ref[:, cols:] + 0.5 * jnp.where(even, near, far)
    pair = [first.astype(jnp.bfloat16), final.astype(jnp.bfloat16)]
    bands = dot(waves_ref[...], jnp.concatenate(pair, axis=1)).astype(jnp.bfloat16)
    bands_ref[...] = bands
    core = core_ref[...] + dot_t(bands, bands)
    packed = pack(core)
    half = packed.shape[0] // 2
    low = parity(tile, tile_count) == 0
    kept_ref[...] = jnp.where(low, packed[:half], packed[half:])
    given_ref[...] = jnp.where(low, packed[half:], packed[:half])


def outer(tile_count, edge, near, this, that, waves, core):
    count = waves.shape[0]
    half = jax.ShapeDtypeStruct((count // 12 * 5, count // 3 * 2), jnp.float32)
    return pl.pallas_call(
        functools.partial(outer_kernel, tile_count),
        out_shape=[jax.ShapeDtypeStruct((count, edge.shape[1]), jnp.bfloat16), half, half],
        in_specs=[VMEM] * 6,
        out_specs=[VMEM] * 3,
        compiler_params=pltpu.CompilerParams(vmem_limit_bytes=16 * MIB),
        name="outer",
    )(edge, near, this, that, waves, core)


def summed(kept, given, axis, beside):
    count = lax.axis_size(axis)
    kept = kept + lax.ppermute(given, axis, partners(count, 1))
    mask, first = 2, True
    while mask < count:
        kept = kept + lax.ppermute(kept, axis, partners(count, mask + 1))
        if first:
            kept, *beside = lax.optimization_barrier((kept, *beside))
        mask, first = mask * 2, False
    return kept, lax.ppermute(kept, axis, partners(count, 1)), beside


def lane(v, j):
    return jnp.take_along_axis(v, jnp.full(v.shape, j, jnp.int32), axis=1)


def row(v, k):
    return jnp.take_along_axis(v, jnp.full(v.shape, k, jnp.int32), axis=0)


def assembled(rows, place):
    strips = []
    for s in range(0, len(rows), 8):
        strip = rows[s]
        for k in range(1, 8):
            strip = jnp.where(place == k, rows[s + k], strip)
        strips.append(strip)
    return jnp.concatenate(strips, axis=0)


def inverse_factor(crossed):
    size = crossed.shape[0]
    ids = [lax.broadcasted_iota(jnp.int32, (size, size), d) for d in range(2)]
    eye = (ids[0] == ids[1]).astype(jnp.float32)
    joined = jnp.concatenate([crossed, eye], axis=1)
    strips = [joined[s : s + 8] for s in range(0, size, 8)]
    place = lax.broadcasted_iota(jnp.int32, strips[0].shape, 0)
    rows, early = [], []
    for start in range(0, size, WIDE):
        first = start // 8
        cols = early + [
            [lane(s, start + k) for s in strips[first:]] for k in range(len(early), WIDE)
        ]
        ahead = range(start + WIDE, min(size, start + WIDE + EARLY))
        early = [[lane(s, j) for s in strips[first:]] for j in ahead]
        for k in range(0, WIDE, 2):
            q, s = k // 8, k % 8
            a, b, c = row(cols[k][q], s), row(cols[k][q], s + 1), row(cols[k + 1][q], s + 1)
            inv_a = pl.reciprocal(a, approx=True)
            m = b * inv_a
            pivot = c - b * m
            inv_c = pl.reciprocal(pivot, approx=True)
            below = place > s + 1
            u = [jnp.where(below, cols[k][q], 0.0)] + cols[k][q + 1 :]
            v = [jnp.where(below, cols[k + 1][q], 0.0)] + cols[k + 1][q + 1 :]
            v = [j - i * m for i, j in zip(u, v)]

            def eliminate(target, offset):
                top, low = row(target[offset], s), row(target[offset], s + 1)
                low = low - top * m
                x, y = top * inv_a, low * inv_c
                for i in range(len(u)):
                    target[offset + i] = (target[offset + i] - u[i] * x) - v[i] * y
                return top, low

            for later in cols[k + 2 :] + early:
                eliminate(later, q)
            top, low = eliminate(strips, first + q)
            rows += [top * lax.rsqrt(a), low * lax.rsqrt(pivot)]
        early = [col[WIDE // 8 :] for col in early]
    return assembled(rows, place)


def stacked(a, b):
    size = a.shape[1] // 2
    left = lax.broadcasted_iota(jnp.int32, a.shape, 1) < size
    high, middle, low = thirds(jnp.where(left, pltpu.roll(a, size, 1), a))
    two = jnp.where(left, high, middle)
    by_high, by_middle, by_low = thirds(b)
    return [
        (
            jnp.concatenate([two, jnp.where(left, high, low)], axis=1),
            jnp.concatenate([by_high, by_high, by_middle, by_high], axis=0),
        ),
        (two, jnp.concatenate([by_low, by_middle], axis=0)),
    ]


def inverse_dot(inverse, b):
    (a, x), (c, y) = stacked(inverse, b)
    return dot(a, x) + dot(c, y)


def project_kernel(
    scale,
    tile_count,
    kept_ref,
    other_ref,
    start_ref,
    table_ref,
    waves_ref,
    inside_ref,
    edges_ref,
    out_hbm,
    flat_ref,
    out_ref,
    sems,
):
    hour_count, row_count, cols = out_ref.shape
    kept, other = kept_ref[...], other_ref[...]
    low = parity(lax.axis_index("tile"), tile_count) == 0
    blocks = jnp.concatenate([jnp.where(low, kept, other), jnp.where(low, other, kept)], axis=0)
    core = unpack(blocks * scale)
    waves = waves_ref[...]

    def by_waves(x):
        high, middle, rest = (dot(part, waves) for part in thirds(x))
        return high + (middle + rest)

    panel = by_waves(exact_dot(start_ref[...], core))
    crossed = exact_dot_t(panel, panel)
    table = table_ref[...]
    high, middle, rest = (dot(table, part) for part in thirds(by_waves(core)))
    gram = high + (middle + rest)
    for sweep in range(ITERS):
        inverse = inverse_factor(crossed)
        if sweep < ITERS - 1:
            panel = inverse_dot(inverse, exact_dot(panel, gram))
            crossed = exact_dot_t(panel, panel)
    basis_t = inverse_dot(inverse, panel)
    basis = basis_t.T.astype(jnp.bfloat16)
    basis_t = basis_t.astype(jnp.bfloat16)
    parts = [(inside_ref[:, i * cols : (i + 2) * cols], i + 1, i + 2) for i in range(0, row_count - 2, 2)]
    parts.append((edges_ref[...], 0, row_count - 1))
    parts = [(dot(basis_t, part).astype(jnp.bfloat16), rows) for part, *rows in parts]
    steps = sems.shape[0]
    hours = hour_count // steps
    flat = hours * row_count
    copies = []
    for step in range(steps):
        part = slice(step * hours, (step + 1) * hours)
        for coefficients, rows in parts:
            rebuilt = dot(basis[part], coefficients)
            for k, i in enumerate(rows):
                to = pl.ds(step * flat + i, hours, stride=row_count)
                flat_ref[to] = rebuilt[:, k * cols : (k + 1) * cols]
        whole = flat_ref[step * flat : (step + 1) * flat]
        out_ref[part] = whole.reshape(hours, row_count, cols).astype(jnp.bfloat16)
        copies.append(pltpu.make_async_copy(out_ref.at[part], out_hbm.at[part], sems.at[step]))
        copies[-1].start()
    for copy in copies:
        copy.wait()


def project(kept, other, start, table, waves, inside, edges, scale, shape):
    hour_count, row_count, cols = shape
    return pl.pallas_call(
        functools.partial(project_kernel, scale, lax.axis_size("tile")),
        out_shape=jax.ShapeDtypeStruct(shape, jnp.bfloat16),
        in_specs=[VMEM] * 7,
        out_specs=HBM,
        scratch_shapes=[
            pltpu.VMEM((hour_count * row_count, cols), jnp.float32),
            pltpu.VMEM(shape, jnp.bfloat16),
            pltpu.SemaphoreType.DMA((OUT_STEPS,)),
        ],
        compiler_params=pltpu.CompilerParams(vmem_limit_bytes=16 * MIB),
        name="project",
    )(kept, other, start, table, waves, inside, edges)


def body(flux_east, flux_north, band_freqs, start_basis):
    hour_count, row_count, col_count = flux_east.shape
    tile_count = lax.axis_size("tile")
    cell_total = row_count * col_count * tile_count
    scale = (2.0 / hour_count) ** 2 / cell_total
    even = lax.axis_index("tile") % 2 == 0
    head, tail = flux_east[:, 0], flux_east[:, -1]
    near, far = jnp.where(even, tail, head), jnp.where(even, head, tail)
    this = lax.ppermute(far, "tile", across_pairs(tile_count, 0))
    that = lax.ppermute(far, "tile", across_pairs(tile_count, 1))
    near = lax.ppermute(near, "tile", partners(tile_count, 1))
    bands, core, edge, table, waves = inner(band_freqs[None], flux_east, flux_north)
    start = jnp.dot(start_basis.T, waves.T.astype(jnp.float32), precision=lax.Precision.HIGHEST)
    edge_bands, kept, given = outer(tile_count, edge, near, this, that, waves, core)
    bands, given = lax.optimization_barrier((bands, given))

    def filtered(part):
        product = jnp.dot(table, part, preferred_element_type=jnp.float32)
        return (product * (2.0 / hour_count)).astype(jnp.bfloat16)

    beside = [filtered(bands), filtered(edge_bands), start]
    kept, other, (inside, edges, start) = summed(kept, given, "tile", beside)
    shape = flux_east.shape
    return project(kept, other, start, table, waves, inside, edges, scale, shape)


def solution(mesh):
    placed = (P(None, ("grp", "tile"), None), P(None, ("grp", "tile"), None), P(), P())
    return jax.shard_map(
        body, mesh=mesh, in_specs=placed, out_specs=P(None, ("grp", "tile"), None), check_vma=False
    )
```
